32 devices in a mesh: groups: 2 (over y), bank: 4 (over x, core), query: 4 (over z).
Axes of the slice: x: 2, y: 2, z: 4, core: 2. Of those that a mesh axis runs over, the one named last changes fastest.
Arguments:
- queries: bfloat16 [256, 768], P(('groups', 'bank', 'query')), parts along dimension 0, may hold values from -12 to 12
- bank_keys: bfloat16 [65536, 768], P(('groups', 'bank', 'query')), parts along dimension 0, may hold values from -5 to 5
- bank_labels: bfloat16 [65536, 1000], P(('groups', 'bank', 'query')), parts along dimension 0, may hold values from 0.0009994507 to 1
Outputs:
- log_votes: float32 [256, 1000], P(('groups', 'bank', 'query')), parts along dimension 0
The draws below stay inside these ranges and needn't reach their ends.
There are 2 independent parts, one for each index of `groups`. The reference program is written for one: setup_inputs(seed, part) draws one part's arguments, and reference() takes and returns one part's arrays. A program takes and returns all parts, laid end to end along the dimension named above; each array names one. Nothing has to cross between parts.
All inputs are finite; a program needn't handle non-finite values.
Results may differ from the reference program's by a relative error of at most 0.0003.
Values may be sent and summed in bfloat16 or wider, within the bound.
No kernel may reach another device: no remote copies, remote signals or barrier semaphores. Data moves between devices by JAX's collectives and lax.ppermute only.
A program may use at most 64 MiB of HBM per device.

```python
import math
import jax
import jax.numpy as jnp
from jax import lax

E = 768
C = 1000
B_DEV = 2048
NQ = 128
NB = 32768
N_BANK = 4
N_QUERY = 4


def draw_queries(key, part):
    key = jax.random.fold_in(key, 11)
    values = jnp.clip(jax.random.normal(key, (NQ, E), jnp.float32), -4.0, 4.0)
    return values.astype(jnp.bfloat16)


def draw_bank_keys(key, part):
    key = jax.random.fold_in(key, 12)
    values = jnp.clip(jax.random.normal(key, (NB, E), jnp.float32), -4.0, 4.0)
    return values.astype(jnp.bfloat16)


def block_scale(key, extent, pieces, smallest, top_value):
    gain, own = 1.0, jax.random.fold_in(key, 6)
    for dim, parts in pieces:
        steps = jnp.exp(jax.random.uniform(jax.random.fold_in(own, dim), (parts,), jnp.float32, smallest / len(pieces), top_value / len(pieces)))
        gain = gain * jnp.repeat(steps, extent[dim] // parts).reshape([-1 if axis == dim else 1 for axis in range(len(extent))])
    return gain


def setup_inputs(seed: int = 0, part: int = 0) -> dict:
    key_of = jax.random.split(jax.random.key(seed), 4)
    own_keys = jax.random.split(jax.random.fold_in(key_of[3], part), 4)
    queries = draw_queries(jax.random.fold_in(jax.random.fold_in(key_of[3], part), 71), part)
    bank_keys = draw_bank_keys(jax.random.fold_in(jax.random.fold_in(key_of[3], part), 71), part)
    bank_labels = jnp.clip(jnp.exp(math.log(1.0) - 6.9083047 * jax.random.uniform(own_keys[2], (NB, C), jnp.float32) ** block_scale(own_keys[2], (NB, C), ((0, 16),), -0.2, 0.2)), 0.0009994507, 1.0).astype(jnp.bfloat16)
    return {"queries": queries, "bank_keys": bank_keys, "bank_labels": bank_labels}


SCORE_GAIN = 3.0

def partial_stats(query_rows, key_block, label_block):
    score_gain = SCORE_GAIN / math.sqrt(query_rows.shape[1])
    scores = lax.dot_general(query_rows, key_block, (((1,), (1,)), ((), ())), preferred_element_type=jnp.float32) * score_gain
    peaks = lax.optimization_barrier(jnp.max(scores, axis=1))
    weights = jnp.exp(scores - peaks[:, None])
    totals = lax.optimization_barrier(jnp.sum(weights, axis=1))
    votes = jnp.dot(weights.astype(jnp.bfloat16), label_block, preferred_element_type=jnp.float32)
    return (peaks, totals, votes)

def reference(queries, bank_keys, bank_labels):
    shards = N_BANK * N_QUERY
    key_blocks = bank_keys.reshape(shards, B_DEV, E)
    label_blocks = bank_labels.reshape(shards, B_DEV, C)

    def absorb(running, blocks):
        row_top, denominator, class_mass = running
        peaks, totals, votes = partial_stats(queries, blocks[0], blocks[1])
        new_top = jnp.maximum(row_top, peaks)
        old_factor = jnp.exp(row_top - new_top)
        new_factor = jnp.exp(peaks - new_top)
        denominator = denominator * old_factor + totals * new_factor
        class_mass = class_mass * old_factor[:, None] + votes * new_factor[:, None]
        return ((new_top, denominator, class_mass), None)
    initial = (jnp.full((NQ,), -jnp.inf, jnp.float32), jnp.zeros((NQ,), jnp.float32), jnp.zeros((NQ, C), jnp.float32))
    final, unused = lax.scan(absorb, initial, (key_blocks, label_blocks))
    return jnp.log(final[2] / final[1][:, None])
```

```python
import functools
import math

import jax
import jax.numpy as jnp
from jax import lax
from jax.experimental import pallas as pl
from jax.experimental.pallas import tpu as pltpu
from jax.sharding import PartitionSpec as P

SCORE_GAIN = 3.0
AXES = ("bank", "query")
LANES = 128
VMEM = pl.BlockSpec(memory_space=pltpu.VMEM)


def pad_lanes(width):
    return -(-(width + 2) // LANES) * LANES


def stats_kernel(q_ref, k_ref, lt_ref, keep_ref, send_ref):
    rows, width = q_ref.shape
    classes = lt_ref.shape[0]
    half = rows // 2
    scores = lax.dot_general(
        q_ref[...], k_ref[...], (((1,), (1,)), ((), ())), preferred_element_type=jnp.float32
    ) * (SCORE_GAIN / math.sqrt(width))
    peaks = jnp.max(scores, axis=1, keepdims=True)
    weights = jnp.exp(scores - peaks)
    totals = jnp.sum(weights, axis=1, keepdims=True)
    votes = lax.dot_general(
        weights.astype(jnp.bfloat16),
        lt_ref[...],
        (((1,), (1,)), ((), ())),
        preferred_element_type=jnp.float32,
    )
    for ref, lo in ((keep_ref, 0), (send_ref, half)):
        ref[:, :classes] = votes[lo : lo + half]
        ref[:, classes : classes + 1] = peaks[lo : lo + half]
        ref[:, classes + 1 : classes + 2] = totals[lo : lo + half]


def stats(queries, keys, labels_t):
    rows, width = queries.shape
    bank = keys.shape[0]
    classes = labels_t.shape[0]
    out = jax.ShapeDtypeStruct((rows // 2, pad_lanes(classes)), jnp.float32)
    return pl.pallas_call(
        stats_kernel,
        out_shape=(out, out),
        in_specs=[VMEM] * 3,
        out_specs=(VMEM, VMEM),
        compiler_params=pltpu.CompilerParams(vmem_limit_bytes=32 * 1024 * 1024),
        cost_estimate=pl.CostEstimate(
            flops=2 * rows * bank * (width + classes),
            bytes_accessed=2 * bank * (width + classes),
            transcendentals=rows * bank,
        ),
    )(queries, keys, labels_t)


def combine(mine, other, classes):
    peak_a, peak_b = mine[:, classes : classes + 1], other[:, classes : classes + 1]
    top = jnp.maximum(peak_a, peak_b)
    factor_a, factor_b = jnp.exp(peak_a - top), jnp.exp(peak_b - top)
    return top, factor_a * mine + factor_b * other


def merge_kernel(classes, mine_ref, other_ref, keep_ref, send_ref):
    half = keep_ref.shape[0]
    for ref, lo in ((keep_ref, 0), (send_ref, half)):
        top, merged = combine(mine_ref[lo : lo + half], other_ref[lo : lo + half], classes)
        ref[...] = merged
        ref[:, classes : classes + 1] = top


def merge(mine, other, classes):
    out = jax.ShapeDtypeStruct((mine.shape[0] // 2, mine.shape[1]), jnp.float32)
    return pl.pallas_call(
        functools.partial(merge_kernel, classes),
        out_shape=(out, out),
        in_specs=[VMEM] * 2,
        out_specs=(VMEM, VMEM),
    )(mine, other)


def finish_kernel(classes, mine_ref, other_ref, out_ref):
    _, merged = combine(mine_ref[...], other_ref[...], classes)
    out_ref[...] = jnp.log(merged[:, :classes] / merged[:, classes + 1 : classes + 2])


def finish(mine, other, classes):
    return pl.pallas_call(
        functools.partial(finish_kernel, classes),
        out_shape=jax.ShapeDtypeStruct((mine.shape[0], classes), jnp.float32),
        in_specs=[VMEM] * 2,
        out_specs=VMEM,
    )(mine, other)


def local(bits, size, queries, bank_keys, bank_labels):
    def swap(block, bit):
        return lax.ppermute(block, AXES, [(i, i ^ bit) for i in range(size)])

    classes = bank_labels.shape[1]
    rows = queries
    for bit in bits:
        rows = jnp.concatenate([rows, swap(rows, bit)], axis=0)
    keep, send = stats(rows, bank_keys, bank_labels.T)
    for bit in bits[:0:-1]:
        keep, send = merge(keep, swap(send, bit), classes)
    return finish(keep, swap(send, bits[0]), classes)


def solution(mesh):
    placed = P(("groups", "bank", "query"), None)
    size = mesh.shape["bank"] * mesh.shape["query"]
    query_bits = [1 << b for b in range(mesh.shape["query"].bit_length() - 1)]
    bank_bits = [mesh.shape["query"] << b for b in range(mesh.shape["bank"].bit_length() - 1)]
    bits = query_bits + bank_bits[1:] + bank_bits[:1]
    return jax.shard_map(
        functools.partial(local, bits, size),
        mesh=mesh,
        in_specs=(placed,) * 3,
        out_specs=placed,
        check_vma=False,
    )
```

```python
import functools
import math

import jax
import jax.numpy as jnp
from jax import lax
from jax.experimental import pallas as pl
from jax.experimental.pallas import tpu as pltpu
from jax.sharding import PartitionSpec as P

SCORE_GAIN = 3.0
AXES = ("bank", "query")
LANES = 128
VMEM = pl.BlockSpec(memory_space=pltpu.VMEM)


MIB = 1 << 20


def pad_lanes(width):
    return -(-(width + 2) // LANES) * LANES


def grant(*arrays):
    return pltpu.CompilerParams(
        vmem_limit_bytes=sum(2 * math.prod(a.shape) * a.dtype.itemsize for a in arrays) + MIB
    )


def join_kernel(a_ref, b_ref, out_ref):
    rows = a_ref.shape[0]
    out_ref[:rows] = a_ref[...]
    out_ref[rows:] = b_ref[...]


def join(a, b):
    out = jax.ShapeDtypeStruct((2 * a.shape[0], a.shape[1]), a.dtype)
    return pl.pallas_call(
        join_kernel,
        out_shape=out,
        in_specs=[VMEM] * 2,
        out_specs=VMEM,
        compiler_params=grant(out, out),
    )(a, b)


def stats_kernel(near_ref, far_ref, k_ref, lt_ref, keep_ref, send_ref):
    half, width = near_ref.shape
    classes = lt_ref.shape[0]
    queries = jnp.concatenate([near_ref[...], far_ref[...]], axis=0)
    scores = lax.dot_general(
        queries, k_ref[...], (((1,), (1,)), ((), ())), preferred_element_type=jnp.float32
    ) * (SCORE_GAIN / math.sqrt(width))
    peaks = jnp.max(scores, axis=1, keepdims=True)
    weights = jnp.exp(scores - peaks)
    totals = jnp.sum(weights, axis=1, keepdims=True)
    votes = lax.dot_general(
        weights.astype(jnp.bfloat16),
        lt_ref[...],
        (((1,), (1,)), ((), ())),
        preferred_element_type=jnp.float32,
    )
    for ref, lo in ((keep_ref, 0), (send_ref, half)):
        ref[:, :classes] = votes[lo : lo + half]
        ref[:, classes : classes + 1] = peaks[lo : lo + half]
        ref[:, classes + 1 : classes + 2] = totals[lo : lo + half]


def stats(near, far, keys, labels_t):
    rows, width = 2 * near.shape[0], near.shape[1]
    bank = keys.shape[0]
    classes = labels_t.shape[0]
    out = jax.ShapeDtypeStruct((rows // 2, pad_lanes(classes)), jnp.float32)
    scores = jax.ShapeDtypeStruct((rows, bank), jnp.float32)
    return pl.pallas_call(
        stats_kernel,
        out_shape=(out, out),
        in_specs=[VMEM] * 4,
        out_specs=(VMEM, VMEM),
        compiler_params=grant(near, far, keys, labels_t, out, out, scores),
        cost_estimate=pl.CostEstimate(
            flops=2 * rows * bank * (width + classes),
            bytes_accessed=2 * bank * (width + classes),
            transcendentals=rows * bank,
        ),
    )(near, far, keys, labels_t)


def combine(mine, other, classes):
    peak_a, peak_b = mine[:, classes : classes + 1], other[:, classes : classes + 1]
    top = jnp.maximum(peak_a, peak_b)
    factor_a, factor_b = jnp.exp(peak_a - top), jnp.exp(peak_b - top)
    return top, factor_a * mine + factor_b * other


def merge_kernel(classes, mine_ref, other_ref, keep_ref, send_ref):
    half = keep_ref.shape[0]
    for ref, lo in ((keep_ref, 0), (send_ref, half)):
        top, merged = combine(mine_ref[lo : lo + half], other_ref[lo : lo + half], classes)
        ref[...] = merged
        ref[:, classes : classes + 1] = top


def merge(mine, other, classes):
    out = jax.ShapeDtypeStruct((mine.shape[0] // 2, mine.shape[1]), jnp.float32)
    return pl.pallas_call(
        functools.partial(merge_kernel, classes),
        out_shape=(out, out),
        in_specs=[VMEM] * 2,
        out_specs=(VMEM, VMEM),
        compiler_params=grant(mine, other, out, out),
    )(mine, other)


def finish_kernel(classes, mine_ref, other_ref, out_ref):
    _, merged = combine(mine_ref[...], other_ref[...], classes)
    out_ref[...] = jnp.log(merged[:, :classes] / merged[:, classes + 1 : classes + 2])


def finish(mine, other, classes):
    out = jax.ShapeDtypeStruct((mine.shape[0], classes), jnp.float32)
    return pl.pallas_call(
        functools.partial(finish_kernel, classes),
        out_shape=out,
        in_specs=[VMEM] * 2,
        out_specs=VMEM,
        compiler_params=grant(mine, other, out),
    )(mine, other)


def local(bits, size, queries, bank_keys, bank_labels):
    def swap(block, bit):
        return lax.ppermute(block, AXES, [(i, i ^ bit) for i in range(size)])

    classes = bank_labels.shape[1]
    rows = queries
    for bit in bits[:-1]:
        rows = join(rows, swap(rows, bit))
    keep, send = stats(rows, swap(rows, bits[-1]), bank_keys, bank_labels.T)
    for bit in bits[:0:-1]:
        keep, send = merge(keep, swap(send, bit), classes)
    return finish(keep, swap(send, bits[0]), classes)


def solution(mesh):
    placed = P(("groups", "bank", "query"), None)
    size = mesh.shape["bank"] * mesh.shape["query"]
    query_bits = [1 << b for b in range(mesh.shape["query"].bit_length() - 1)]
    bank_bits = [mesh.shape["query"] << b for b in range(mesh.shape["bank"].bit_length() - 1)]
    bits = query_bits + bank_bits[1:] + bank_bits[:1]
    return jax.shard_map(
        functools.partial(local, bits, size),
        mesh=mesh,
        in_specs=(placed,) * 3,
        out_specs=placed,
        check_vma=False,
    )
```

```python
import functools
import math

import jax
import jax.numpy as jnp
from jax import lax
from jax.experimental import pallas as pl
from jax.experimental.pallas import tpu as pltpu
from jax.sharding import PartitionSpec as P

SCORE_GAIN = 3.0
AXES = ("bank", "query")
LANES = 128
VMEM = pl.BlockSpec(memory_space=pltpu.VMEM)


MIB = 1 << 20


def pad_lanes(width):
    return -(-(width + 2) // LANES) * LANES


def grant(*arrays):
    return pltpu.CompilerParams(
        vmem_limit_bytes=sum(2 * math.prod(a.shape) * a.dtype.itemsize for a in arrays) + MIB
    )


BESIDE = pl.CostEstimate(flops=4_000_000_000, bytes_accessed=1 << 17, transcendentals=0)


def fetch_kernel(a_ref, out_ref):
    out_ref[...] = a_ref[...]


def fetch(a):
    return pl.pallas_call(
        fetch_kernel,
        out_shape=jax.ShapeDtypeStruct(a.shape, a.dtype),
        in_specs=[VMEM],
        out_specs=VMEM,
        compiler_params=grant(a, a),
        cost_estimate=BESIDE,
    )(a)


def join_kernel(a_ref, b_ref, out_ref):
    rows = a_ref.shape[0]
    out_ref[:rows] = a_ref[...]
    out_ref[rows:] = b_ref[...]


def join(a, b):
    out = jax.ShapeDtypeStruct((2 * a.shape[0], a.shape[1]), a.dtype)
    return pl.pallas_call(
        join_kernel,
        out_shape=out,
        in_specs=[VMEM] * 2,
        out_specs=VMEM,
        compiler_params=grant(out, out),
        cost_estimate=BESIDE,
    )(a, b)


def stats_kernel(near_ref, far_ref, k_ref, lt_ref, keep_ref, send_ref):
    half, width = near_ref.shape
    classes = lt_ref.shape[0]
    queries = jnp.concatenate([near_ref[...], far_ref[...]], axis=0)
    scores = lax.dot_general(
        queries, k_ref[...], (((1,), (1,)), ((), ())), preferred_element_type=jnp.float32
    ) * (SCORE_GAIN / math.sqrt(width))
    peaks = jnp.max(scores, axis=1, keepdims=True)
    weights = jnp.exp(scores - peaks)
    totals = jnp.sum(weights, axis=1, keepdims=True)
    votes = lax.dot_general(
        weights.astype(jnp.bfloat16),
        lt_ref[...],
        (((1,), (1,)), ((), ())),
        preferred_element_type=jnp.float32,
    )
    for ref, lo in ((keep_ref, 0), (send_ref, half)):
        ref[:, :classes] = votes[lo : lo + half]
        ref[:, classes : classes + 1] = peaks[lo : lo + half]
        ref[:, classes + 1 : classes + 2] = totals[lo : lo + half]


def stats(near, far, keys, labels_t):
    rows, width = 2 * near.shape[0], near.shape[1]
    bank = keys.shape[0]
    classes = labels_t.shape[0]
    out = jax.ShapeDtypeStruct((rows // 2, pad_lanes(classes)), jnp.float32)
    scores = jax.ShapeDtypeStruct((rows, bank), jnp.float32)
    return pl.pallas_call(
        stats_kernel,
        out_shape=(out, out),
        in_specs=[VMEM] * 4,
        out_specs=(VMEM, VMEM),
        compiler_params=grant(near, far, keys, labels_t, out, out, scores),
        cost_estimate=pl.CostEstimate(
            flops=2 * rows * bank * (width + classes),
            bytes_accessed=2 * bank * (width + classes),
            transcendentals=rows * bank,
        ),
    )(near, far, keys, labels_t)


def combine(mine, other, classes):
    peak_a, peak_b = mine[:, classes : classes + 1], other[:, classes : classes + 1]
    top = jnp.maximum(peak_a, peak_b)
    factor_a, factor_b = jnp.exp(peak_a - top), jnp.exp(peak_b - top)
    return top, factor_a * mine + factor_b * other


def merge_kernel(classes, mine_ref, other_ref, keep_ref, send_ref):
    half = keep_ref.shape[0]
    for ref, lo in ((keep_ref, 0), (send_ref, half)):
        top, merged = combine(mine_ref[lo : lo + half], other_ref[lo : lo + half], classes)
        ref[...] = merged
        ref[:, classes : classes + 1] = top


def merge(mine, other, classes):
    out = jax.ShapeDtypeStruct((mine.shape[0] // 2, mine.shape[1]), jnp.float32)
    return pl.pallas_call(
        functools.partial(merge_kernel, classes),
        out_shape=(out, out),
        in_specs=[VMEM] * 2,
        out_specs=(VMEM, VMEM),
        compiler_params=grant(mine, other, out, out),
    )(mine, other)


def finish_kernel(classes, mine_ref, other_ref, out_ref):
    _, merged = combine(mine_ref[...], other_ref[...], classes)
    out_ref[...] = jnp.log(merged[:, :classes] / merged[:, classes + 1 : classes + 2])


def finish(mine, other, classes):
    out = jax.ShapeDtypeStruct((mine.shape[0], classes), jnp.float32)
    return pl.pallas_call(
        functools.partial(finish_kernel, classes),
        out_shape=out,
        in_specs=[VMEM] * 2,
        out_specs=VMEM,
        compiler_params=grant(mine, other, out),
    )(mine, other)


def local(bits, size, queries, bank_keys, bank_labels):
    def swap(block, bit):
        return lax.ppermute(block, AXES, [(i, i ^ bit) for i in range(size)])

    classes = bank_labels.shape[1]
    rows = join(fetch(queries), swap(queries, bits[0]))
    for bit in bits[1:-1]:
        rows = join(rows, swap(rows, bit))
    keep, send = stats(rows, swap(rows, bits[-1]), bank_keys, bank_labels.T)
    for bit in bits[:0:-1]:
        keep, send = merge(keep, swap(send, bit), classes)
    return finish(keep, swap(send, bits[0]), classes)


def solution(mesh):
    placed = P(("groups", "bank", "query"), None)
    size = mesh.shape["bank"] * mesh.shape["query"]
    query_bits = [1 << b for b in range(mesh.shape["query"].bit_length() - 1)]
    bank_bits = [mesh.shape["query"] << b for b in range(mesh.shape["bank"].bit_length() - 1)]
    bits = query_bits[::-1] + bank_bits[1:] + bank_bits[:1]
    return jax.shard_map(
        functools.partial(local, bits, size),
        mesh=mesh,
        in_specs=(placed,) * 3,
        out_specs=placed,
        check_vma=False,
    )
```

```python
import functools
import math

import jax
import jax.numpy as jnp
from jax import lax
from jax.experimental import pallas as pl
from jax.experimental.pallas import tpu as pltpu
from jax.sharding import PartitionSpec as P

SCORE_GAIN = 3.0
AXES = ("bank", "query")
LANES = 128
MIB = 1 << 20
VMEM = pl.BlockSpec(memory_space=pltpu.VMEM)
BESIDE = pl.CostEstimate(flops=4_000_000_000, bytes_accessed=1 << 17, transcendentals=0)


def grant(*arrays):
    return pltpu.CompilerParams(
        vmem_limit_bytes=sum(2 * math.prod(a.shape) * a.dtype.itemsize for a in arrays) + MIB
    )


def call(kernel, outs, *args, scratch=(), cost=None):
    return pl.pallas_call(
        kernel,
        out_shape=outs,
        in_specs=[VMEM] * len(args),
        out_specs=jax.tree.map(lambda _: VMEM, outs),
        compiler_params=grant(*args, *jax.tree.leaves(outs), *scratch),
        cost_estimate=cost,
    )(*args)


def fetch_kernel(a_ref, out_ref):
    out_ref[...] = a_ref[...]


def fetch(a):
    return call(fetch_kernel, jax.ShapeDtypeStruct(a.shape, a.dtype), a, cost=BESIDE)


def join_kernel(a_ref, b_ref, out_ref):
    rows = a_ref.shape[0]
    out_ref[:rows] = a_ref[...]
    out_ref[rows:] = b_ref[...]


def join(a, b):
    out = jax.ShapeDtypeStruct((2 * a.shape[0], a.shape[1]), a.dtype)
    return call(join_kernel, out, a, b, cost=BESIDE)


def record_shape(rows, classes):
    return jax.ShapeDtypeStruct((rows, -(-(classes + 2) // LANES) * LANES), jnp.float32)


def parts_of(record, classes):
    return (
        record[:, classes : classes + 1],
        record[:, classes + 1 : classes + 2],
        record[:, :classes],
    )


def combine(*parts):
    top = functools.reduce(jnp.maximum, [peak for peak, _, _ in parts])
    factors = [jnp.exp(peak - top) for peak, _, _ in parts]
    total = sum(f * t for f, (_, t, _) in zip(factors, parts))
    votes = sum(f * v for f, (_, _, v) in zip(factors, parts))
    return top, total, votes


def put(ref, row, parts):
    peak, total, votes = parts
    rows, classes = votes.shape
    at = slice(row, row + rows)
    ref[at, :classes] = votes
    spare = ref.shape[1] - classes
    column = lax.broadcasted_iota(jnp.int32, (rows, spare), 1)
    ref[at, classes:] = jnp.where(column == 0, peak, jnp.where(column == 1, total, 0.0))


def stats_kernel(own_ref, near_ref, far_ref, across_ref, k_ref, lt_ref, keep_ref, send_ref):
    count, width = own_ref.shape
    half = count // 2
    queries = jnp.concatenate(
        [own_ref[...], near_ref[...], far_ref[...], across_ref[...]], axis=0
    )
    scores = lax.dot_general(
        queries, k_ref[...], (((1,), (1,)), ((), ())), preferred_element_type=jnp.float32
    ) * (SCORE_GAIN / math.sqrt(width))
    peaks = jnp.max(scores, axis=1, keepdims=True)
    weights = jnp.exp(scores - peaks)
    totals = jnp.sum(weights, axis=1, keepdims=True)
    votes = lax.dot_general(
        weights.astype(jnp.bfloat16),
        lt_ref[...],
        (((1,), (1,)), ((), ())),
        preferred_element_type=jnp.float32,
    )

    def move(ref, row, start, rows):
        at = slice(start, start + rows)
        put(ref, row, (peaks[at], totals[at], votes[at]))

    move(keep_ref, 0, 0, half)
    move(send_ref, 0, half, half)
    move(keep_ref, half, count, half)
    move(send_ref, half, count + half, half)
    move(keep_ref, count, 2 * count, count)
    move(send_ref, count, 3 * count, count)


def stats(blocks, keys, labels_t):
    rows, width = 4 * blocks[0].shape[0], keys.shape[1]
    bank, classes = keys.shape[0], labels_t.shape[0]
    out = record_shape(rows // 2, classes)
    scores = jax.ShapeDtypeStruct((rows, bank), jnp.float32)
    cost = pl.CostEstimate(
        flops=2 * rows * bank * (width + classes),
        bytes_accessed=2 * bank * (width + classes),
        transcendentals=rows * bank,
    )
    return call(
        stats_kernel, (out, out), *blocks, keys, labels_t, scratch=(scores,), cost=cost
    )


def merge_kernel(classes, mine_ref, other_ref, keep_ref, send_ref):
    half = keep_ref.shape[0] // 4
    for quarter in range(4):
        for ref, lo in ((keep_ref, 0), (send_ref, half)):
            at = slice(2 * quarter * half + lo, 2 * quarter * half + lo + half)
            both = [parts_of(r[at], classes) for r in (mine_ref, other_ref)]
            put(ref, quarter * half, combine(*both))


def merge(mine, other, classes):
    out = record_shape(mine.shape[0] // 2, classes)
    return call(functools.partial(merge_kernel, classes), (out, out), mine, other)


def split_kernel(classes, mine_ref, other_ref, own_ref, near_ref, far_ref):
    rows = own_ref.shape[0]
    both = [parts_of(r[...], classes) for r in (mine_ref, other_ref)]
    peak, total, votes = combine(*both)
    for ref, lo, count in ((own_ref, 0, rows), (near_ref, rows, rows), (far_ref, 2 * rows, 2 * rows)):
        at = slice(lo, lo + count)
        put(ref, 0, (peak[at], total[at], votes[at]))


def split(mine, other, classes):
    rows = mine.shape[0] // 4
    outs = (
        record_shape(rows, classes),
        record_shape(rows, classes),
        record_shape(2 * rows, classes),
    )
    return call(functools.partial(split_kernel, classes), outs, mine, other)


def tail_kernel(a_ref, out_ref):
    out_ref[...] = a_ref[out_ref.shape[0] :]


def tail(a):
    out = jax.ShapeDtypeStruct((a.shape[0] // 2, a.shape[1]), a.dtype)
    return call(tail_kernel, out, a)


def finish_kernel(classes, own_ref, near_ref, far_ref, across_ref, out_ref):
    rows = out_ref.shape[0]
    refs = (own_ref, near_ref, far_ref, across_ref)
    _, total, votes = combine(*[parts_of(r[:rows], classes) for r in refs])
    out_ref[...] = jnp.log(votes / total)


def finish(own, near, far, across, classes):
    out = jax.ShapeDtypeStruct((own.shape[0], classes), jnp.float32)
    return call(functools.partial(finish_kernel, classes), out, own, near, far, across)


def local(size, core, lead, queries, bank_keys, bank_labels):
    def swap(block, bit):
        return lax.ppermute(block, AXES, [(i, i ^ bit) for i in range(size)])

    def swap_far(block):
        return lax.ppermute(block, AXES, [(i, i ^ (2 if i & core else 3)) for i in range(size)])

    classes = bank_labels.shape[1]
    first, *rest = [*lead, core]
    own = join(fetch(queries), swap(queries, first))
    for bit in rest:
        own = join(own, swap(own, bit))
    far = swap_far(own)
    near = swap(own, 1)
    across = swap(far, core)
    keep, send = stats((own, near, far, across), bank_keys, bank_labels.T)
    came = swap(send, core)
    for bit in lead[::-1]:
        keep, send = merge(keep, came, classes)
        came = swap(send, bit)
    own, near, far = split(keep, came, classes)
    far = swap_far(far)
    near = swap(near, 1)
    across = swap(tail(far), core)
    return finish(own, near, far, across, classes)


def solution(mesh):
    placed = P(("groups", "bank", "query"), None)
    query, bank = mesh.shape["query"], mesh.shape["bank"]
    lead = [1 << b for b in range(2, query.bit_length() - 1)]
    lead += [query << b for b in range(1, bank.bit_length() - 1)]
    return jax.shard_map(
        functools.partial(local, query * bank, query, lead),
        mesh=mesh,
        in_specs=(placed,) * 3,
        out_specs=placed,
        check_vma=False,
    )
```

```python
import functools
import math

import jax
import jax.numpy as jnp
from jax import lax
from jax.experimental import pallas as pl
from jax.experimental.pallas import tpu as pltpu
from jax.sharding import PartitionSpec as P

SCORE_GAIN = 3.0
AXES = ("bank", "query")
LANES = 128
POWER, CENTRE = 24.0, 5.0
MIB = 1 << 20
VMEM = pl.BlockSpec(memory_space=pltpu.VMEM)
BESIDE = pl.CostEstimate(flops=4_000_000_000, bytes_accessed=1 << 17, transcendentals=0)


def grant(*arrays):
    return pltpu.CompilerParams(
        vmem_limit_bytes=sum(2 * math.prod(a.shape) * a.dtype.itemsize for a in arrays) + MIB
    )


def call(kernel, outs, *args, scratch=(), cost=None):
    return pl.pallas_call(
        kernel,
        out_shape=outs,
        in_specs=[VMEM] * len(args),
        out_specs=jax.tree.map(lambda _: VMEM, outs),
        compiler_params=grant(*args, *jax.tree.leaves(outs), *scratch),
        cost_estimate=cost,
    )(*args)


def fetch_kernel(a_ref, out_ref):
    out_ref[...] = a_ref[...]


def fetch(a):
    return call(fetch_kernel, jax.ShapeDtypeStruct(a.shape, a.dtype), a, cost=BESIDE)


def join_kernel(a_ref, b_ref, out_ref):
    rows = a_ref.shape[0]
    out_ref[:rows] = a_ref[...]
    out_ref[rows:] = b_ref[...]


def join(a, b):
    out = jax.ShapeDtypeStruct((2 * a.shape[0], a.shape[1]), a.dtype)
    return call(join_kernel, out, a, b, cost=BESIDE)


def record_shape(rows, classes, dtype=jnp.float32):
    return jax.ShapeDtypeStruct((rows, -(-(classes + 6) // LANES) * LANES), dtype)


def columns(block, start, count):
    return [block[:, c : c + 1] for c in range(start, start + count)]


def parts_of(record, classes):
    peak, total = columns(record, classes, 2)
    return peak, total, record[:, :classes]


def write(ref, votes, extra):
    rows, classes = votes.shape
    spare = ref.shape[1] - classes
    column = lax.broadcasted_iota(jnp.int32, (rows, spare), 1)
    after = jnp.zeros((rows, spare), jnp.float32)
    for c, values in enumerate(extra):
        after = jnp.where(column == c, values, after)
    ref[...] = jnp.concatenate([votes, after], axis=1).astype(ref.dtype)


def pieces(x):
    high = x.astype(jnp.bfloat16).astype(jnp.float32)
    middle = (x - high).astype(jnp.bfloat16).astype(jnp.float32)
    return [high, middle, x - high - middle]


def encode(ref, parts):
    peak, total, votes = parts
    code = jnp.exp2(POWER * jnp.log2(votes) + POWER * (CENTRE - jnp.log2(total)))
    write(ref, code, pieces(peak) + pieces(total))


def decode(block, classes):
    record = block.astype(jnp.float32)
    p = columns(record, classes, 6)
    peak, total = p[0] + p[1] + p[2], p[3] + p[4] + p[5]
    log = jnp.log2(record[:, :classes]) * (1 / POWER)
    return peak, total, jnp.exp2(log + (jnp.log2(total) - CENTRE))


def combine(*parts):
    top = functools.reduce(jnp.maximum, [peak for peak, _, _ in parts])
    factors = [jnp.exp(peak - top) for peak, _, _ in parts]
    total = sum(f * t for f, (_, t, _) in zip(factors, parts))
    votes = sum(f * v for f, (_, _, v) in zip(factors, parts))
    return top, total, votes


def rows_of(parts, *ranges):
    return tuple(jnp.concatenate([x[lo:hi] for lo, hi in ranges], axis=0) for x in parts)


def stats_kernel(own_ref, near_ref, far_ref, across_ref, k_ref, lt_ref, keep_ref, send_ref):
    count, width = own_ref.shape
    half = count // 2
    queries = jnp.concatenate(
        [own_ref[...], near_ref[...], far_ref[...], across_ref[...]], axis=0
    )
    scores = lax.dot_general(
        queries, k_ref[...], (((1,), (1,)), ((), ())), preferred_element_type=jnp.float32
    ) * (SCORE_GAIN / math.sqrt(width))
    peaks = jnp.max(scores, axis=1, keepdims=True)
    weights = jnp.exp(scores - peaks)
    totals = jnp.sum(weights, axis=1, keepdims=True)
    votes = lax.dot_general(
        weights.astype(jnp.bfloat16),
        lt_ref[...],
        (((1,), (1,)), ((), ())),
        preferred_element_type=jnp.float32,
    )

    parts = (peaks, totals, votes)
    keep = rows_of(parts, (0, half), (count, count + half), (2 * count, 3 * count))
    send = rows_of(parts, (half, count), (count + half, 2 * count), (3 * count, 4 * count))
    write(keep_ref, keep[2], keep[:2])
    encode(send_ref, send)


def stats(blocks, keys, labels_t):
    rows, width = 4 * blocks[0].shape[0], keys.shape[1]
    bank, classes = keys.shape[0], labels_t.shape[0]
    outs = (record_shape(rows // 2, classes), record_shape(rows // 2, classes, jnp.bfloat16))
    scores = jax.ShapeDtypeStruct((rows, bank), jnp.float32)
    cost = pl.CostEstimate(
        flops=2 * rows * bank * (width + classes),
        bytes_accessed=2 * bank * (width + classes),
        transcendentals=rows * bank,
    )
    return call(
        stats_kernel, outs, *blocks, keys, labels_t, scratch=(scores,), cost=cost
    )


def merge_kernel(classes, mine_ref, other_ref, keep_ref, send_ref):
    half = keep_ref.shape[0] // 4
    starts = range(0, 8 * half, 2 * half)
    parts = combine(parts_of(mine_ref[...], classes), decode(other_ref[...], classes))
    keep = rows_of(parts, *[(lo, lo + half) for lo in starts])
    send = rows_of(parts, *[(lo + half, lo + 2 * half) for lo in starts])
    write(keep_ref, keep[2], keep[:2])
    encode(send_ref, send)


def merge(mine, other, classes):
    rows = mine.shape[0] // 2
    outs = (record_shape(rows, classes), record_shape(rows, classes, jnp.bfloat16))
    return call(functools.partial(merge_kernel, classes), outs, mine, other)


def split_kernel(classes, mine_ref, other_ref, own_ref, near_ref, far_ref):
    rows = own_ref.shape[0]
    parts = combine(parts_of(mine_ref[...], classes), decode(other_ref[...], classes))
    own = rows_of(parts, (0, rows))
    write(own_ref, own[2], own[:2])
    encode(near_ref, rows_of(parts, (rows, 2 * rows)))
    encode(far_ref, rows_of(parts, (2 * rows, 4 * rows)))


def split(mine, other, classes):
    rows = mine.shape[0] // 4
    outs = (
        record_shape(rows, classes),
        record_shape(rows, classes, jnp.bfloat16),
        record_shape(2 * rows, classes, jnp.bfloat16),
    )
    return call(functools.partial(split_kernel, classes), outs, mine, other)


def tail_kernel(a_ref, out_ref):
    out_ref[...] = a_ref[...].astype(jnp.float32)[out_ref.shape[0] :].astype(out_ref.dtype)


def tail(a):
    out = jax.ShapeDtypeStruct((a.shape[0] // 2, a.shape[1]), a.dtype)
    return call(tail_kernel, out, a)


def finish_kernel(classes, own_ref, near_ref, far_ref, across_ref, out_ref):
    rows = out_ref.shape[0]
    came = [decode(r[...], classes) for r in (near_ref, far_ref, across_ref)]
    came[1] = rows_of(came[1], (0, rows))
    _, total, votes = combine(parts_of(own_ref[...], classes), *came)
    out_ref[...] = jnp.log(votes / total)


def finish(own, near, far, across, classes):
    out = jax.ShapeDtypeStruct((own.shape[0], classes), jnp.float32)
    return call(functools.partial(finish_kernel, classes), out, own, near, far, across)


def local(size, core, lead, queries, bank_keys, bank_labels):
    def swap(block, bit):
        return lax.ppermute(block, AXES, [(i, i ^ bit) for i in range(size)])

    def swap_far(block):
        return lax.ppermute(block, AXES, [(i, i ^ (2 if i & core else 3)) for i in range(size)])

    classes = bank_labels.shape[1]
    first, *rest = [*lead, core]
    own = join(fetch(queries), swap(queries, first))
    for bit in rest:
        own = join(own, swap(own, bit))
    far = swap_far(own)
    near = swap(own, 1)
    across = swap(far, core)
    keep, send = stats((own, near, far, across), bank_keys, bank_labels.T)
    came = swap(send, core)
    for bit in lead[::-1]:
        keep, send = merge(keep, came, classes)
        came = swap(send, bit)
    own, near, far = split(keep, came, classes)
    far = swap_far(far)
    near = swap(near, 1)
    across = swap(tail(far), core)
    return finish(own, near, far, across, classes)


def solution(mesh):
    placed = P(("groups", "bank", "query"), None)
    query, bank = mesh.shape["query"], mesh.shape["bank"]
    lead = [1 << b for b in range(2, query.bit_length() - 1)]
    lead += [query << b for b in range(1, bank.bit_length() - 1)]
    return jax.shard_map(
        functools.partial(local, query * bank, query, lead),
        mesh=mesh,
        in_specs=(placed,) * 3,
        out_specs=placed,
        check_vma=False,
    )
```

```python
import functools
import math

import jax
import jax.numpy as jnp
from jax import lax
from jax.experimental import pallas as pl
from jax.experimental.pallas import tpu as pltpu
from jax.sharding import PartitionSpec as P

SCORE_GAIN = 3.0
AXES = ("bank", "query")
LANES = 128
POWER, CENTRE = 24.0, 5.0
MIB = 1 << 20
VMEM = pl.BlockSpec(memory_space=pltpu.VMEM)
BESIDE = pl.CostEstimate(flops=4_000_000_000, bytes_accessed=1 << 17, transcendentals=0)


def grant(*arrays):
    return pltpu.CompilerParams(
        vmem_limit_bytes=sum(2 * math.prod(a.shape) * a.dtype.itemsize for a in arrays) + MIB
    )


def call(kernel, outs, *args, scratch=(), cost=None):
    return pl.pallas_call(
        kernel,
        out_shape=outs,
        in_specs=[VMEM] * len(args),
        out_specs=jax.tree.map(lambda _: VMEM, outs),
        compiler_params=grant(*args, *jax.tree.leaves(outs), *scratch),
        cost_estimate=cost,
    )(*args)


def fetch_kernel(a_ref, out_ref):
    out_ref[...] = a_ref[...]


def fetch(a):
    return call(fetch_kernel, jax.ShapeDtypeStruct(a.shape, a.dtype), a, cost=BESIDE)


def join_kernel(a_ref, b_ref, out_ref):
    rows = a_ref.shape[0]
    out_ref[:rows] = a_ref[...]
    out_ref[rows:] = b_ref[...]


def join(a, b):
    out = jax.ShapeDtypeStruct((2 * a.shape[0], a.shape[1]), a.dtype)
    return call(join_kernel, out, a, b, cost=BESIDE)


def record_shape(rows, classes, dtype=jnp.float32):
    return jax.ShapeDtypeStruct((rows, -(-(classes + 6) // LANES) * LANES), dtype)


def columns(block, start, count):
    return [block[:, c : c + 1] for c in range(start, start + count)]


def parts_of(record, classes):
    peak, total = columns(record, classes, 2)
    return peak, total, record[:, :classes]


def write(ref, votes, extra):
    rows, classes = votes.shape
    spare = ref.shape[1] - classes
    column = lax.broadcasted_iota(jnp.int32, (rows, spare), 1)
    after = jnp.zeros((rows, spare), jnp.float32)
    for c, values in enumerate(extra):
        after = jnp.where(column == c, values, after)
    ref[...] = jnp.concatenate([votes, after], axis=1).astype(ref.dtype)


def pieces(x):
    high = x.astype(jnp.bfloat16).astype(jnp.float32)
    middle = (x - high).astype(jnp.bfloat16).astype(jnp.float32)
    return [high, middle, x - high - middle]


def encode(ref, parts):
    peak, total, votes = parts
    code = jnp.exp2(POWER * jnp.log2(votes) + POWER * (CENTRE - jnp.log2(total)))
    write(ref, code, pieces(peak) + pieces(total))


def decode(block, classes):
    record = block.astype(jnp.float32)
    p = columns(record, classes, 6)
    peak, total = p[0] + p[1] + p[2], p[3] + p[4] + p[5]
    log = jnp.log2(record[:, :classes]) * (1 / POWER)
    return peak, total, jnp.exp2(log + (jnp.log2(total) - CENTRE))


def combine(*parts):
    top = functools.reduce(jnp.maximum, [peak for peak, _, _ in parts])
    factors = [jnp.exp(peak - top) for peak, _, _ in parts]
    total = sum(f * t for f, (_, t, _) in zip(factors, parts))
    votes = sum(f * v for f, (_, _, v) in zip(factors, parts))
    return top, total, votes


def rows_of(parts, *ranges):
    return tuple(jnp.concatenate([x[lo:hi] for lo, hi in ranges], axis=0) for x in parts)


def stats_kernel(unit, own_ref, near_ref, far_ref, across_ref, k_ref, lt_ref, keep_ref, send_ref):
    count, width = own_ref.shape
    half = count // 2
    queries = jnp.concatenate(
        [own_ref[...], near_ref[...], far_ref[...], across_ref[...]], axis=0
    )
    scores = lax.dot_general(
        queries, k_ref[...], (((1,), (1,)), ((), ())), preferred_element_type=jnp.float32
    ) * (SCORE_GAIN / math.sqrt(width))
    peaks = jnp.max(scores, axis=1, keepdims=True)
    weights = jnp.exp(scores - peaks)
    totals = jnp.sum(weights, axis=1, keepdims=True)
    votes = lax.dot_general(
        weights.astype(jnp.bfloat16),
        lt_ref[...],
        (((1,), (1,)), ((), ())),
        preferred_element_type=jnp.float32,
    )

    slots = half // unit
    keep, send = [], []
    for block in range(4):
        odd = [n.bit_count() % 2 for n in range(slots)]
        same = [block * count + (n + slots * o) * unit for n, o in enumerate(odd)]
        other = [block * count + (n + slots * (1 - o)) * unit for n, o in enumerate(odd)]
        (send if block == 3 else keep).extend(same)
        (keep if block == 2 else send).extend(other)
    parts = (peaks, totals, votes)
    keep, send = (rows_of(parts, *[(lo, lo + unit) for lo in los]) for los in (keep, send))
    write(keep_ref, keep[2], keep[:2])
    encode(send_ref, send)


def stats(blocks, keys, labels_t, unit):
    rows, width = 4 * blocks[0].shape[0], keys.shape[1]
    bank, classes = keys.shape[0], labels_t.shape[0]
    outs = (record_shape(rows // 2, classes), record_shape(rows // 2, classes, jnp.bfloat16))
    scores = jax.ShapeDtypeStruct((rows, bank), jnp.float32)
    cost = pl.CostEstimate(
        flops=2 * rows * bank * (width + classes),
        bytes_accessed=2 * bank * (width + classes),
        transcendentals=rows * bank,
    )
    return call(
        functools.partial(stats_kernel, unit), outs, *blocks, keys, labels_t, scratch=(scores,), cost=cost
    )


def merge_kernel(classes, mine_ref, other_ref, keep_ref, send_ref):
    half = keep_ref.shape[0] // 4
    starts = range(0, 8 * half, 2 * half)
    parts = combine(parts_of(mine_ref[...], classes), decode(other_ref[...], classes))
    keep = rows_of(parts, *[(lo, lo + half) for lo in starts])
    send = rows_of(parts, *[(lo + half, lo + 2 * half) for lo in starts])
    write(keep_ref, keep[2], keep[:2])
    encode(send_ref, send)


def merge(mine, other, classes):
    rows = mine.shape[0] // 2
    outs = (record_shape(rows, classes), record_shape(rows, classes, jnp.bfloat16))
    return call(functools.partial(merge_kernel, classes), outs, mine, other)


def split_kernel(classes, mine_ref, other_ref, own_ref, near_ref, far_ref):
    rows = own_ref.shape[0]
    parts = combine(parts_of(mine_ref[...], classes), decode(other_ref[...], classes))
    own = rows_of(parts, (0, rows))
    write(own_ref, own[2], own[:2])
    encode(near_ref, rows_of(parts, (rows, 2 * rows)))
    encode(far_ref, rows_of(parts, (2 * rows, 4 * rows)))


def split(mine, other, classes):
    rows = mine.shape[0] // 4
    outs = (
        record_shape(rows, classes),
        record_shape(rows, classes, jnp.bfloat16),
        record_shape(2 * rows, classes, jnp.bfloat16),
    )
    return call(functools.partial(split_kernel, classes), outs, mine, other)


def tail_kernel(a_ref, out_ref):
    out_ref[...] = a_ref[...].astype(jnp.float32)[out_ref.shape[0] :].astype(out_ref.dtype)


def tail(a):
    out = jax.ShapeDtypeStruct((a.shape[0] // 2, a.shape[1]), a.dtype)
    return call(tail_kernel, out, a)


def finish_kernel(classes, own_ref, near_ref, far_ref, across_ref, out_ref):
    rows = out_ref.shape[0]
    came = [decode(r[...], classes) for r in (near_ref, far_ref, across_ref)]
    came[1] = rows_of(came[1], (0, rows))
    _, total, votes = combine(parts_of(own_ref[...], classes), *came)
    out_ref[...] = jnp.log(votes / total)


def finish(own, near, far, across, classes):
    out = jax.ShapeDtypeStruct((own.shape[0], classes), jnp.float32)
    return call(functools.partial(finish_kernel, classes), out, own, near, far, across)


def local(size, core, lead, queries, bank_keys, bank_labels):
    def swap(block, bit):
        return lax.ppermute(block, AXES, [(i, i ^ bit) for i in range(size)])

    def swap_far(block):
        return lax.ppermute(block, AXES, [(i, i ^ (3 if i & core else 2)) for i in range(size)])

    classes = bank_labels.shape[1]
    first, *rest = [bit ^ core for bit in lead] + [core]
    own = join(fetch(queries), swap(queries, first))
    for bit in rest:
        own = join(own, swap(own, bit))
    far = swap_far(own)
    near = swap(own, 1 ^ core)
    across = swap(far, core)
    keep, send = stats((own, near, far, across), bank_keys, bank_labels.T, queries.shape[0])
    came = swap(send, core)
    for bit in lead[::-1]:
        keep, send = merge(keep, came, classes)
        came = swap(send, bit)
    own, near, far = split(keep, came, classes)
    far = swap_far(far)
    near = swap(near, 1 ^ core)
    across = swap(tail(far), core)
    return finish(own, near, far, across, classes)


def solution(mesh):
    placed = P(("groups", "bank", "query"), None)
    query, bank = mesh.shape["query"], mesh.shape["bank"]
    lead = [1 << b for b in range(2, query.bit_length() - 1)]
    lead += [query << b for b in range(1, bank.bit_length() - 1)]
    return jax.shard_map(
        functools.partial(local, query * bank, query, lead),
        mesh=mesh,
        in_specs=(placed,) * 3,
        out_specs=placed,
        check_vma=False,
    )
```

```python
import functools
import math

import jax
import jax.numpy as jnp
from jax import lax
from jax.experimental import pallas as pl
from jax.experimental.pallas import tpu as pltpu
from jax.sharding import PartitionSpec as P

SCORE_GAIN = 3.0
AXES = ("bank", "query")
LANES = 128
POWER, CENTRE = 24.0, 5.0
MIB = 1 << 20
VMEM = pl.BlockSpec(memory_space=pltpu.VMEM)
BESIDE = pl.CostEstimate(flops=4_000_000_000, bytes_accessed=1 << 17, transcendentals=0)


def grant(*arrays):
    return pltpu.CompilerParams(
        vmem_limit_bytes=sum(2 * math.prod(a.shape) * a.dtype.itemsize for a in arrays) + MIB
    )


def call(kernel, outs, *args, scratch=(), cost=None):
    return pl.pallas_call(
        kernel,
        out_shape=outs,
        in_specs=[VMEM] * len(args),
        out_specs=jax.tree.map(lambda _: VMEM, outs),
        compiler_params=grant(*args, *jax.tree.leaves(outs), *scratch),
        cost_estimate=cost,
    )(*args)


def fetch_kernel(a_ref, out_ref):
    out_ref[...] = a_ref[...]


def fetch(a):
    return call(fetch_kernel, jax.ShapeDtypeStruct(a.shape, a.dtype), a, cost=BESIDE)


def join_kernel(a_ref, b_ref, out_ref):
    rows = a_ref.shape[0]
    out_ref[:rows] = a_ref[...]
    out_ref[rows:] = b_ref[...]


def join(a, b):
    out = jax.ShapeDtypeStruct((2 * a.shape[0], a.shape[1]), a.dtype)
    return call(join_kernel, out, a, b, cost=BESIDE)


def record_shape(rows, classes, dtype=jnp.float32):
    return jax.ShapeDtypeStruct((rows, -(-(classes + 6) // LANES) * LANES), dtype)


def columns(block, start, count):
    return [block[:, c : c + 1] for c in range(start, start + count)]


def parts_of(record, classes):
    peak, total = columns(record, classes, 2)
    return peak, total, record[:, :classes]


def write(ref, votes, extra):
    rows, classes = votes.shape
    spare = ref.shape[1] - classes
    column = lax.broadcasted_iota(jnp.int32, (rows, spare), 1)
    after = jnp.zeros((rows, spare), jnp.float32)
    for c, values in enumerate(extra):
        after = jnp.where(column == c, values, after)
    ref[...] = jnp.concatenate([votes, after], axis=1).astype(ref.dtype)


def pieces(x):
    high = x.astype(jnp.bfloat16).astype(jnp.float32)
    middle = (x - high).astype(jnp.bfloat16).astype(jnp.float32)
    return [high, middle, x - high - middle]


def encode(ref, parts):
    peak, total, votes = parts
    code = jnp.exp2(POWER * jnp.log2(votes) + POWER * (CENTRE - jnp.log2(total)))
    write(ref, code, pieces(peak) + pieces(total))


def decode(block, classes):
    record = block.astype(jnp.float32)
    p = columns(record, classes, 6)
    peak, total = p[0] + p[1] + p[2], p[3] + p[4] + p[5]
    log = jnp.log2(record[:, :classes]) * (1 / POWER)
    return peak, total, jnp.exp2(log + (jnp.log2(total) - CENTRE))


def combine(*parts):
    top = functools.reduce(jnp.maximum, [peak for peak, _, _ in parts])
    factors = [jnp.exp(peak - top) for peak, _, _ in parts]
    total = sum(f * t for f, (_, t, _) in zip(factors, parts))
    votes = sum(f * v for f, (_, _, v) in zip(factors, parts))
    return top, total, votes


def rows_of(parts, *ranges):
    return tuple(jnp.concatenate([x[lo:hi] for lo, hi in ranges], axis=0) for x in parts)


def stats_kernel(unit, own_ref, near_ref, far_ref, across_ref, k_ref, lt_ref, keep_ref, send_ref):
    count, width = own_ref.shape
    half = count // 2
    queries = jnp.concatenate(
        [own_ref[...], near_ref[...], far_ref[...], across_ref[...]], axis=0
    )
    scores = lax.dot_general(
        queries, k_ref[...], (((1,), (1,)), ((), ())), preferred_element_type=jnp.float32
    ) * (SCORE_GAIN / math.sqrt(width))
    peaks = jnp.max(scores, axis=1, keepdims=True)
    weights = jnp.exp(scores - peaks)
    totals = jnp.sum(weights, axis=1, keepdims=True)
    votes = lax.dot_general(
        weights.astype(jnp.bfloat16),
        lt_ref[...],
        (((1,), (1,)), ((), ())),
        preferred_element_type=jnp.float32,
    )

    slots = half // unit
    odd = [n.bit_count() % 2 for n in range(slots)]

    def rows(block, n, other_core):
        return block * count + (n + slots * (other_core ^ odd[n])) * unit

    keep = [rows(block, n, odd[n]) for block in (0, 1) for n in range(slots)]
    send = [rows(block, n, 1 ^ odd[n]) for block in (0, 1) for n in range(slots)]
    for other_core in (0, 1):
        keep += [rows(2 + odd[n], n, other_core) for n in range(slots)]
        send += [rows(3 - odd[n], n, other_core) for n in range(slots)]
    parts = (peaks, totals, votes)
    keep, send = (rows_of(parts, *[(lo, lo + unit) for lo in los]) for los in (keep, send))
    write(keep_ref, keep[2], keep[:2])
    encode(send_ref, send)


def stats(blocks, keys, labels_t, unit):
    rows, width = 4 * blocks[0].shape[0], keys.shape[1]
    bank, classes = keys.shape[0], labels_t.shape[0]
    outs = (record_shape(rows // 2, classes), record_shape(rows // 2, classes, jnp.bfloat16))
    scores = jax.ShapeDtypeStruct((rows, bank), jnp.float32)
    cost = pl.CostEstimate(
        flops=2 * rows * bank * (width + classes),
        bytes_accessed=2 * bank * (width + classes),
        transcendentals=rows * bank,
    )
    return call(
        functools.partial(stats_kernel, unit), outs, *blocks, keys, labels_t, scratch=(scores,), cost=cost
    )


def merge_kernel(classes, mine_ref, other_ref, keep_ref, send_ref):
    half = keep_ref.shape[0] // 4
    starts = range(0, 8 * half, 2 * half)
    parts = combine(parts_of(mine_ref[...], classes), decode(other_ref[...], classes))
    keep = rows_of(parts, *[(lo, lo + half) for lo in starts])
    send = rows_of(parts, *[(lo + half, lo + 2 * half) for lo in starts])
    write(keep_ref, keep[2], keep[:2])
    encode(send_ref, send)


def merge(mine, other, classes):
    rows = mine.shape[0] // 2
    outs = (record_shape(rows, classes), record_shape(rows, classes, jnp.bfloat16))
    return call(functools.partial(merge_kernel, classes), outs, mine, other)


def split_kernel(classes, mine_ref, other_ref, own_ref, near_ref, far_ref):
    rows = own_ref.shape[0]
    parts = combine(parts_of(mine_ref[...], classes), decode(other_ref[...], classes))
    own = rows_of(parts, (0, rows))
    write(own_ref, own[2], own[:2])
    encode(near_ref, rows_of(parts, (rows, 2 * rows)))
    encode(far_ref, rows_of(parts, (2 * rows, 4 * rows)))


def split(mine, other, classes):
    rows = mine.shape[0] // 4
    outs = (
        record_shape(rows, classes),
        record_shape(rows, classes, jnp.bfloat16),
        record_shape(2 * rows, classes, jnp.bfloat16),
    )
    return call(functools.partial(split_kernel, classes), outs, mine, other)


def tail_kernel(a_ref, out_ref):
    out_ref[...] = a_ref[...].astype(jnp.float32)[out_ref.shape[0] :].astype(out_ref.dtype)


def tail(a):
    out = jax.ShapeDtypeStruct((a.shape[0] // 2, a.shape[1]), a.dtype)
    return call(tail_kernel, out, a)


def finish_kernel(classes, own_ref, near_ref, far_ref, across_ref, out_ref):
    rows = out_ref.shape[0]
    came = [decode(r[...], classes) for r in (near_ref, far_ref, across_ref)]
    came[1] = rows_of(came[1], (0, rows))
    _, total, votes = combine(parts_of(own_ref[...], classes), *came)
    out_ref[...] = jnp.log(votes / total)


def finish(own, near, far, across, classes):
    out = jax.ShapeDtypeStruct((own.shape[0], classes), jnp.float32)
    return call(functools.partial(finish_kernel, classes), out, own, near, far, across)


def local(size, core, lead, queries, bank_keys, bank_labels):
    def swap(block, bit):
        return lax.ppermute(block, AXES, [(i, i ^ bit) for i in range(size)])

    def swap_far(block):
        return lax.ppermute(block, AXES, [(i, i ^ (3 if i & core else 2)) for i in range(size)])

    classes = bank_labels.shape[1]
    first, *rest = [bit ^ core for bit in lead] + [core]
    own = join(fetch(queries), swap(queries, first))
    for bit in rest:
        own = join(own, swap(own, bit))
    far = swap_far(own)
    near = swap(own, 1 ^ core)
    across = swap(far, core)
    keep, send = stats((own, near, far, across), bank_keys, bank_labels.T, queries.shape[0])
    came = swap(send, core)
    for bit in lead[::-1]:
        keep, send = merge(keep, came, classes)
        came = swap(send, bit ^ core)
    own, near, far = split(keep, came, classes)
    far = swap_far(far)
    near = swap(near, 1 ^ core)
    across = swap(tail(far), core)
    return finish(own, near, far, across, classes)


def solution(mesh):
    placed = P(("groups", "bank", "query"), None)
    query, bank = mesh.shape["query"], mesh.shape["bank"]
    lead = [1 << b for b in range(2, query.bit_length() - 1)]
    lead += [query << b for b in range(1, bank.bit_length() - 1)]
    return jax.shard_map(
        functools.partial(local, query * bank, query, lead),
        mesh=mesh,
        in_specs=(placed,) * 3,
        out_specs=placed,
        check_vma=False,
    )
```

```python
import functools
import math

import jax
import jax.numpy as jnp
from jax import lax
from jax.experimental import pallas as pl
from jax.experimental.pallas import tpu as pltpu
from jax.sharding import PartitionSpec as P

SCORE_GAIN = 3.0
AXES = ("bank", "query")
LANES = 128
POWER, CENTRE = 24.0, 5.0
MIB = 1 << 20
VMEM = pl.BlockSpec(memory_space=pltpu.VMEM)
BESIDE = pl.CostEstimate(flops=4_000_000_000, bytes_accessed=1 << 17, transcendentals=0)


def grant(*arrays):
    return pltpu.CompilerParams(
        vmem_limit_bytes=sum(2 * math.prod(a.shape) * a.dtype.itemsize for a in arrays) + MIB
    )


def call(kernel, outs, *args, scratch=(), cost=None):
    return pl.pallas_call(
        kernel,
        out_shape=outs,
        in_specs=[VMEM] * len(args),
        out_specs=jax.tree.map(lambda _: VMEM, outs),
        compiler_params=grant(*args, *jax.tree.leaves(outs), *scratch),
        cost_estimate=cost,
    )(*args)


def fetch_kernel(a_ref, out_ref):
    out_ref[...] = a_ref[...]


def fetch(a):
    return call(fetch_kernel, jax.ShapeDtypeStruct(a.shape, a.dtype), a, cost=BESIDE)


def join_kernel(a_ref, b_ref, out_ref):
    rows = a_ref.shape[0]
    out_ref[:rows] = a_ref[...]
    out_ref[rows:] = b_ref[...]


def join(a, b):
    out = jax.ShapeDtypeStruct((2 * a.shape[0], a.shape[1]), a.dtype)
    return call(join_kernel, out, a, b, cost=BESIDE)


def record_shape(rows, classes, dtype=jnp.float32):
    return jax.ShapeDtypeStruct((rows, -(-(classes + 3) // LANES) * LANES), dtype)


def extra_columns(shape, classes, count):
    column = lax.broadcasted_iota(jnp.int32, (shape[0], LANES), 1) + (shape[1] - LANES)
    return [column == classes + c for c in range(count)]


def tiles(record):
    return [record[:, lo : lo + LANES] for lo in range(0, record.shape[1], LANES)]


def log_weight(last, shape, classes, count):
    held = functools.reduce(jnp.logical_or, extra_columns(shape, classes, count))
    return jnp.sum(jnp.where(held, last, 0.0), axis=1, keepdims=True)


def kept(record, classes):
    averages = tiles(record)
    return log_weight(averages[-1], record.shape, classes, 1), averages


def decoded(record, classes):
    codes = tiles(record)
    averages = [jnp.exp2(jnp.log2(c) * (1 / POWER) - CENTRE) for c in codes]
    return log_weight(codes[-1], record.shape, classes, 3), averages


def store(ref, at, averages, classes, extra):
    width = ref.shape[1]
    rows = averages[0].shape[0]
    for lo, values in zip(range(0, width, LANES), averages):
        if lo + LANES == width:
            for held, value in zip(extra_columns((rows, width), classes, len(extra)), extra):
                values = jnp.where(held, value, values)
        ref[at : at + rows, lo : lo + LANES] = values.astype(ref.dtype)


def keep(ref, at, parts, classes):
    store(ref, at, parts[1], classes, [parts[0]])


def encode(ref, at, parts, classes):
    log, averages = parts
    high = log.astype(jnp.bfloat16).astype(jnp.float32)
    middle = (log - high).astype(jnp.bfloat16).astype(jnp.float32)
    codes = [jnp.exp2(POWER * jnp.log2(x) + POWER * CENTRE) for x in averages]
    store(ref, at, codes, classes, [high, middle, log - high - middle])


def combine(*parts):
    top = functools.reduce(jnp.maximum, [log for log, _ in parts])
    weights = [jnp.exp(log - top) for log, _ in parts]
    total = functools.reduce(jnp.add, weights)
    factors = [w / total for w in weights]
    columns = zip(*[averages for _, averages in parts])
    return top + jnp.log(total), [sum(f * x for f, x in zip(factors, c)) for c in columns]


def rows_of(parts, *ranges):
    take = lambda x: jnp.concatenate([x[lo:hi] for lo, hi in ranges], axis=0)
    return take(parts[0]), [take(x) for x in parts[1]]


def stats_kernel(unit, own_ref, near_ref, far_ref, across_ref, k_ref, lt_ref, *out_refs):
    count, width = own_ref.shape
    classes = lt_ref.shape[0]
    half = count // 2
    queries = jnp.concatenate(
        [own_ref[...], near_ref[...], far_ref[...], across_ref[...]], axis=0
    )
    scores = lax.dot_general(
        queries, k_ref[...], (((1,), (1,)), ((), ())), preferred_element_type=jnp.float32
    ) * (SCORE_GAIN / math.sqrt(width))
    peaks = jnp.max(scores, axis=1, keepdims=True)
    weights = jnp.exp(scores - peaks)
    totals = jnp.sum(weights, axis=1, keepdims=True)
    votes = lax.dot_general(
        weights.astype(jnp.bfloat16),
        lt_ref[...],
        (((1,), (1,)), ((), ())),
        preferred_element_type=jnp.float32,
    )

    slots = half // unit
    odd = [n.bit_count() % 2 for n in range(slots)]

    def rows(block, other_core):
        starts = [block * count + (n + slots * (other_core ^ o)) * unit for n, o in enumerate(odd)]
        return [(lo, lo + unit) for lo in starts]

    votes = votes * (1 / totals)
    spare = out_refs[0].shape[1] - classes
    votes = jnp.concatenate([votes, jnp.ones((4 * count, spare), jnp.float32)], axis=1)
    parts = (peaks + jnp.log(totals), tiles(votes))
    far_send, near_send, far_keep, near_keep = out_refs
    encode(far_send, 0, rows_of(parts, *rows(3, 0), *rows(3, 1)), classes)
    encode(near_send, 0, rows_of(parts, *rows(0, 1), *rows(1, 1)), classes)
    keep(far_keep, 0, rows_of(parts, *rows(2, 0), *rows(2, 1)), classes)
    keep(near_keep, 0, rows_of(parts, *rows(0, 0), *rows(1, 0)), classes)


def stats(blocks, keys, labels_t, unit):
    rows, width = 4 * blocks[0].shape[0], keys.shape[1]
    bank, classes = keys.shape[0], labels_t.shape[0]
    outs = [record_shape(rows // 4, classes, d) for d in (jnp.bfloat16, jnp.float32) for _ in range(2)]
    scores = jax.ShapeDtypeStruct((rows, bank), jnp.float32)
    cost = pl.CostEstimate(
        flops=2 * rows * bank * (width + classes),
        bytes_accessed=2 * bank * (width + classes),
        transcendentals=rows * bank,
    )
    return call(
        functools.partial(stats_kernel, unit), outs, *blocks, keys, labels_t, scratch=(scores,), cost=cost
    )


def merge_kernel(put, classes, first, last, mine_ref, other_ref, *out_refs):
    half = mine_ref.shape[0] // 2
    ranges = [(at + first * half // 2, at + last * half // 2) for at in (0, half)]
    mine, other = mine_ref[...], other_ref[...].astype(jnp.float32)

    def merged(ranges):
        a, b = (jnp.concatenate([x[lo:hi] for lo, hi in ranges], axis=0) for x in (mine, other))
        return combine(kept(a, classes), decoded(b, classes))

    for p, ref, chosen in zip(put, out_refs, [[r] for r in ranges] if len(put) > 1 else [ranges]):
        p(ref, 0, merged(chosen), classes)


def merge(mine, other, classes, first, last, *put):
    rows = mine.shape[0] * (last - first) // 2 // len(put)
    outs = [record_shape(rows, classes, jnp.float32 if p is keep else jnp.bfloat16) for p in put]
    kernel = functools.partial(merge_kernel, put, classes, first, last)
    return call(kernel, outs, mine, other)


def tail_kernel(a_ref, out_ref):
    out_ref[...] = a_ref[...].astype(jnp.float32)[out_ref.shape[0] :].astype(out_ref.dtype)


def tail(a):
    out = jax.ShapeDtypeStruct((a.shape[0] // 2, a.shape[1]), a.dtype)
    return call(tail_kernel, out, a)


def finish_kernel(classes, own_ref, near_ref, far_ref, across_ref, out_ref):
    rows = out_ref.shape[0]
    came = [r[...].astype(jnp.float32)[:rows] for r in (near_ref, far_ref, across_ref)]
    _, averages = combine(kept(own_ref[...], classes), *[decoded(r, classes) for r in came])
    out_ref[...] = jnp.concatenate([jnp.log(x) for x in averages], axis=1)[:, :classes]


def finish(own, near, far, across, classes):
    out = jax.ShapeDtypeStruct((own.shape[0], classes), jnp.float32)
    return call(functools.partial(finish_kernel, classes), out, own, near, far, across)


def local(size, core, lead, queries, bank_keys, bank_labels):
    def swap(block, bit):
        return lax.ppermute(block, AXES, [(i, i ^ bit) for i in range(size)])

    def swap_far(block):
        return lax.ppermute(block, AXES, [(i, i ^ (3 if i & core else 2)) for i in range(size)])

    classes = bank_labels.shape[1]
    first, *rest = [bit ^ core for bit in lead] + [core]
    own = join(fetch(queries), swap(queries, first))
    for bit in rest:
        own = join(own, swap(own, bit))
    far = swap_far(own)
    near = swap(own, 1 ^ core)
    across = swap(far, core)
    *sends, far, near = stats((own, near, far, across), bank_keys, bank_labels.T, queries.shape[0])
    far_came, near_came = (swap(send, core) for send in sends)
    for bit in lead[::-1]:
        (send,) = merge(far, far_came, classes, 1, 2, encode)
        (far,) = merge(far, far_came, classes, 0, 1, keep)
        far_came = swap(send, bit)
        (send,) = merge(near, near_came, classes, 1, 2, encode)
        (near,) = merge(near, near_came, classes, 0, 1, keep)
        near_came = swap(send, bit)
    (far,) = merge(far, far_came, classes, 0, 2, encode)
    own, near = merge(near, near_came, classes, 0, 2, keep, encode)
    far = swap_far(far)
    near = swap(near, 1 ^ core)
    across = swap(tail(far), core)
    return finish(own, near, far, across, classes)


def solution(mesh):
    placed = P(("groups", "bank", "query"), None)
    query, bank = mesh.shape["query"], mesh.shape["bank"]
    lead = [1 << b for b in range(2, query.bit_length() - 1)]
    lead += [query << b for b in range(1, bank.bit_length() - 1)]
    return jax.shard_map(
        functools.partial(local, query * bank, query, lead),
        mesh=mesh,
        in_specs=(placed,) * 3,
        out_specs=placed,
        check_vma=False,
    )
```

```python
import functools
import math

import jax
import jax.numpy as jnp
from jax import lax
from jax.experimental import pallas as pl
from jax.experimental.pallas import tpu as pltpu
from jax.sharding import PartitionSpec as P

SCORE_GAIN = 3.0
AXES = ("bank", "query")
LANES = 128
POWER, CENTRE = 24.0, 5.0
MIB = 1 << 20
VMEM = pl.BlockSpec(memory_space=pltpu.VMEM)
BESIDE = pl.CostEstimate(flops=4_000_000_000, bytes_accessed=1 << 17, transcendentals=0)


def grant(*arrays):
    return pltpu.CompilerParams(
        vmem_limit_bytes=sum(2 * math.prod(a.shape) * a.dtype.itemsize for a in arrays) + MIB
    )


def call(kernel, outs, *args, scratch=(), cost=None):
    return pl.pallas_call(
        kernel,
        out_shape=outs,
        in_specs=[VMEM] * len(args),
        out_specs=jax.tree.map(lambda _: VMEM, outs),
        compiler_params=grant(*args, *jax.tree.leaves(outs), *scratch),
        cost_estimate=cost,
    )(*args)


def fetch_kernel(a_ref, out_ref):
    out_ref[...] = a_ref[...]


def fetch(a):
    return call(fetch_kernel, jax.ShapeDtypeStruct(a.shape, a.dtype), a, cost=BESIDE)


def join_kernel(a_ref, b_ref, out_ref):
    rows = a_ref.shape[0]
    out_ref[:rows] = a_ref[...]
    out_ref[rows:] = b_ref[...]


def join(a, b):
    out = jax.ShapeDtypeStruct((2 * a.shape[0], a.shape[1]), a.dtype)
    return call(join_kernel, out, a, b, cost=BESIDE)


def record_shape(rows, classes, dtype=jnp.float32):
    return jax.ShapeDtypeStruct((rows, -(-(classes + 3) // LANES) * LANES), dtype)


def extra_columns(shape, classes, count):
    column = lax.broadcasted_iota(jnp.int32, (shape[0], LANES), 1) + (shape[1] - LANES)
    return [column == classes + c for c in range(count)]


def tiles(record):
    return [record[:, lo : lo + LANES] for lo in range(0, record.shape[1], LANES)]


def log_weight(last, shape, classes, count):
    held = functools.reduce(jnp.logical_or, extra_columns(shape, classes, count))
    return jnp.sum(jnp.where(held, last, 0.0), axis=1, keepdims=True)


def kept(record, classes):
    averages = tiles(record)
    return log_weight(averages[-1], record.shape, classes, 1), averages


def decoded(record, classes):
    codes = tiles(record)
    averages = [jnp.exp2(jnp.log2(c) * (1 / POWER) - CENTRE) for c in codes]
    return log_weight(codes[-1], record.shape, classes, 3), averages


def store(ref, at, averages, classes, extra):
    width = ref.shape[1]
    rows = averages[0].shape[0]
    for lo, values in zip(range(0, width, LANES), averages):
        if lo + LANES == width:
            for held, value in zip(extra_columns((rows, width), classes, len(extra)), extra):
                values = jnp.where(held, value, values)
        ref[at : at + rows, lo : lo + LANES] = values.astype(ref.dtype)


def keep(ref, at, parts, classes):
    store(ref, at, parts[1], classes, [parts[0]])


def encode(ref, at, parts, classes):
    log, averages = parts
    high = log.astype(jnp.bfloat16).astype(jnp.float32)
    middle = (log - high).astype(jnp.bfloat16).astype(jnp.float32)
    codes = [jnp.exp2(POWER * jnp.log2(x) + POWER * CENTRE) for x in averages]
    store(ref, at, codes, classes, [high, middle, log - high - middle])


def combine(*parts):
    top = functools.reduce(jnp.maximum, [log for log, _ in parts])
    weights = [jnp.exp(log - top) for log, _ in parts]
    total = functools.reduce(jnp.add, weights)
    factors = [w / total for w in weights]
    columns = zip(*[averages for _, averages in parts])
    return top + jnp.log(total), [sum(f * x for f, x in zip(factors, c)) for c in columns]


def rows_of(parts, *ranges):
    take = lambda x: jnp.concatenate([x[lo:hi] for lo, hi in ranges], axis=0)
    return take(parts[0]), [take(x) for x in parts[1]]


def stats_kernel(unit, own_ref, near_ref, far_ref, across_ref, k_ref, lt_ref, *out_refs):
    count, width = own_ref.shape
    classes = lt_ref.shape[0]
    half = count // 2
    queries = jnp.concatenate(
        [own_ref[...], near_ref[...], far_ref[...], across_ref[...]], axis=0
    )
    scores = lax.dot_general(
        queries, k_ref[...], (((1,), (1,)), ((), ())), preferred_element_type=jnp.float32
    ) * (SCORE_GAIN / math.sqrt(width))
    peaks = jnp.max(scores, axis=1, keepdims=True)
    weights = jnp.exp(scores - peaks)
    totals = jnp.sum(weights, axis=1, keepdims=True)
    votes = lax.dot_general(
        weights.astype(jnp.bfloat16),
        lt_ref[...],
        (((1,), (1,)), ((), ())),
        preferred_element_type=jnp.float32,
    )

    slots = half // unit
    odd = [n.bit_count() % 2 for n in range(slots)]

    def rows(block, other_core):
        starts = [block * count + (n + slots * (other_core ^ o)) * unit for n, o in enumerate(odd)]
        return [(lo, lo + unit) for lo in starts]

    votes = votes * (1 / totals)
    spare = out_refs[0].shape[1] - classes
    votes = jnp.concatenate([votes, jnp.ones((4 * count, spare), jnp.float32)], axis=1)
    parts = (peaks + jnp.log(totals), tiles(votes))
    far_send, near_send, far_keep, near_keep = out_refs
    encode(far_send, 0, rows_of(parts, *rows(3, 0), *rows(3, 1)), classes)
    encode(near_send, 0, rows_of(parts, *rows(0, 1), *rows(1, 0)), classes)
    keep(far_keep, 0, rows_of(parts, *rows(2, 0), *rows(2, 1)), classes)
    keep(near_keep, 0, rows_of(parts, *rows(0, 0), *rows(1, 1)), classes)


def stats(blocks, keys, labels_t, unit):
    rows, width = 4 * blocks[0].shape[0], keys.shape[1]
    bank, classes = keys.shape[0], labels_t.shape[0]
    outs = [record_shape(rows // 4, classes, d) for d in (jnp.bfloat16, jnp.float32) for _ in range(2)]
    scores = jax.ShapeDtypeStruct((rows, bank), jnp.float32)
    cost = pl.CostEstimate(
        flops=2 * rows * bank * (width + classes),
        bytes_accessed=2 * bank * (width + classes),
        transcendentals=rows * bank,
    )
    return call(
        functools.partial(stats_kernel, unit), outs, *blocks, keys, labels_t, scratch=(scores,), cost=cost
    )


def merge_kernel(put, classes, first, last, mine_ref, other_ref, *out_refs):
    half = mine_ref.shape[0] // 2
    ranges = [(at + first * half // 2, at + last * half // 2) for at in (0, half)]
    mine, other = mine_ref[...], other_ref[...].astype(jnp.float32)

    def merged(ranges):
        a, b = (jnp.concatenate([x[lo:hi] for lo, hi in ranges], axis=0) for x in (mine, other))
        return combine(kept(a, classes), decoded(b, classes))

    for p, ref, chosen in zip(put, out_refs, [[r] for r in ranges] if len(put) > 1 else [ranges]):
        p(ref, 0, merged(chosen), classes)


def merge(mine, other, classes, first, last, *put):
    rows = mine.shape[0] * (last - first) // 2 // len(put)
    outs = [record_shape(rows, classes, jnp.float32 if p is keep else jnp.bfloat16) for p in put]
    kernel = functools.partial(merge_kernel, put, classes, first, last)
    return call(kernel, outs, mine, other)


def tail_kernel(a_ref, out_ref):
    out_ref[...] = a_ref[...].astype(jnp.float32)[out_ref.shape[0] :].astype(out_ref.dtype)


def tail(a):
    out = jax.ShapeDtypeStruct((a.shape[0] // 2, a.shape[1]), a.dtype)
    return call(tail_kernel, out, a)


def finish_kernel(classes, own_ref, near_ref, far_ref, across_ref, out_ref):
    rows = out_ref.shape[0]
    came = [r[...].astype(jnp.float32)[:rows] for r in (near_ref, far_ref, across_ref)]
    _, averages = combine(kept(own_ref[...], classes), *[decoded(r, classes) for r in came])
    out_ref[...] = jnp.concatenate([jnp.log(x) for x in averages], axis=1)[:, :classes]


def finish(own, near, far, across, classes):
    out = jax.ShapeDtypeStruct((own.shape[0], classes), jnp.float32)
    return call(functools.partial(finish_kernel, classes), out, own, near, far, across)


def local(size, core, lead, queries, bank_keys, bank_labels):
    def swap(block, bit):
        return lax.ppermute(block, AXES, [(i, i ^ bit) for i in range(size)])

    def swap_far(block):
        def partner(i):
            inner = (i ^ i >> 1) & 1
            return i ^ 3 if bool(i & core) != bool(inner) else i ^ 2 ^ core

        return lax.ppermute(block, AXES, [(i, partner(i)) for i in range(size)])

    classes = bank_labels.shape[1]
    first, *rest = [bit ^ core for bit in lead] + [core]
    own = join(fetch(queries), swap(queries, first))
    for bit in rest:
        own = join(own, swap(own, bit))
    far = swap_far(own)
    near = swap(own, 1 ^ core)
    across = swap(far, core)
    *sends, far, near = stats((own, near, far, across), bank_keys, bank_labels.T, queries.shape[0])
    far_came, near_came = (swap(send, core) for send in sends)
    for bit in lead[::-1]:
        (send,) = merge(far, far_came, classes, 1, 2, encode)
        (far,) = merge(far, far_came, classes, 0, 1, keep)
        far_came = swap(send, bit)
        (send,) = merge(near, near_came, classes, 1, 2, encode)
        (near,) = merge(near, near_came, classes, 0, 1, keep)
        near_came = swap(send, bit)
    (far,) = merge(far, far_came, classes, 0, 2, encode)
    own, near = merge(near, near_came, classes, 0, 2, keep, encode)
    far = swap_far(far)
    near = swap(near, 1)
    across = swap(tail(far), core)
    return finish(own, near, far, across, classes)


def solution(mesh):
    placed = P(("groups", "bank", "query"), None)
    query, bank = mesh.shape["query"], mesh.shape["bank"]
    lead = [1 << b for b in range(2, query.bit_length() - 1)]
    lead += [query << b for b in range(1, bank.bit_length() - 1)]
    return jax.shard_map(
        functools.partial(local, query * bank, query, lead),
        mesh=mesh,
        in_specs=(placed,) * 3,
        out_specs=placed,
        check_vma=False,
    )
```

```python
import functools
import math

import jax
import jax.numpy as jnp
from jax import lax
from jax.experimental import pallas as pl
from jax.experimental.pallas import tpu as pltpu
from jax.sharding import PartitionSpec as P

SCORE_GAIN = 3.0
AXES = ("bank", "query")
LANES = 128
POWER, CENTRE = 24.0, 5.0
MIB = 1 << 20
VMEM = pl.BlockSpec(memory_space=pltpu.VMEM)
BESIDE = pl.CostEstimate(flops=4_000_000_000, bytes_accessed=1 << 17, transcendentals=0)


def grant(*arrays):
    return pltpu.CompilerParams(
        vmem_limit_bytes=sum(2 * math.prod(a.shape) * a.dtype.itemsize for a in arrays) + MIB
    )


def call(kernel, outs, *args, scratch=(), cost=None):
    return pl.pallas_call(
        kernel,
        out_shape=outs,
        in_specs=[VMEM] * len(args),
        out_specs=jax.tree.map(lambda _: VMEM, outs),
        compiler_params=grant(*args, *jax.tree.leaves(outs), *scratch),
        cost_estimate=cost,
    )(*args)


def fetch_kernel(a_ref, out_ref):
    out_ref[...] = a_ref[...]


def fetch(a):
    return call(fetch_kernel, jax.ShapeDtypeStruct(a.shape, a.dtype), a, cost=BESIDE)


def join_kernel(a_ref, b_ref, out_ref):
    rows = a_ref.shape[0]
    out_ref[:rows] = a_ref[...]
    out_ref[rows:] = b_ref[...]


def join(a, b):
    out = jax.ShapeDtypeStruct((2 * a.shape[0], a.shape[1]), a.dtype)
    return call(join_kernel, out, a, b, cost=BESIDE)


def record_shape(rows, classes, dtype=jnp.float32):
    return jax.ShapeDtypeStruct((rows, -(-(classes + 3) // LANES) * LANES), dtype)


def extra_columns(shape, classes, count):
    column = lax.broadcasted_iota(jnp.int32, (shape[0], LANES), 1) + (shape[1] - LANES)
    return [column == classes + c for c in range(count)]


def tiles(record):
    return [record[:, lo : lo + LANES] for lo in range(0, record.shape[1], LANES)]


def log_weight(last, shape, classes, count):
    held = functools.reduce(jnp.logical_or, extra_columns(shape, classes, count))
    return jnp.sum(jnp.where(held, last, 0.0), axis=1, keepdims=True)


def kept(record, classes):
    averages = tiles(record)
    return log_weight(averages[-1], record.shape, classes, 1), averages


def decoded(record, classes):
    codes = tiles(record)
    averages = [jnp.exp2(jnp.log2(c) * (1 / POWER) - CENTRE) for c in codes]
    return log_weight(codes[-1], record.shape, classes, 3), averages


def store(ref, at, averages, classes, extra):
    width = ref.shape[1]
    rows = averages[0].shape[0]
    for lo, values in zip(range(0, width, LANES), averages):
        if lo + LANES == width:
            for held, value in zip(extra_columns((rows, width), classes, len(extra)), extra):
                values = jnp.where(held, value, values)
        ref[at : at + rows, lo : lo + LANES] = values.astype(ref.dtype)


def keep(ref, at, parts, classes):
    store(ref, at, parts[1], classes, [parts[0]])


def encode(ref, at, parts, classes):
    log, averages = parts
    high = log.astype(jnp.bfloat16).astype(jnp.float32)
    middle = (log - high).astype(jnp.bfloat16).astype(jnp.float32)
    codes = [jnp.exp2(POWER * jnp.log2(x) + POWER * CENTRE) for x in averages]
    store(ref, at, codes, classes, [high, middle, log - high - middle])


def combine(*parts):
    top = functools.reduce(jnp.maximum, [log for log, _ in parts])
    weights = [jnp.exp(log - top) for log, _ in parts]
    total = functools.reduce(jnp.add, weights)
    factors = [w / total for w in weights]
    columns = zip(*[averages for _, averages in parts])
    return top + jnp.log(total), [sum(f * x for f, x in zip(factors, c)) for c in columns]


def rows_of(parts, *ranges):
    take = lambda x: jnp.concatenate([x[lo:hi] for lo, hi in ranges], axis=0)
    return take(parts[0]), [take(x) for x in parts[1]]


def stats_kernel(unit, own_ref, near_ref, far_ref, across_ref, k_ref, lt_ref, *out_refs):
    count, width = own_ref.shape
    classes = lt_ref.shape[0]
    half = count // 2
    queries = jnp.concatenate(
        [own_ref[...], near_ref[...], far_ref[...], across_ref[...]], axis=0
    )
    gain = SCORE_GAIN / math.sqrt(width)
    dot = functools.partial(lax.dot_general, preferred_element_type=jnp.float32)
    by_rows, by_columns = (((1,), (1,)), ((), ())), (((1,), (0,)), ((), ()))
    chunks = [slice(lo, lo + 256) for lo in range(0, k_ref.shape[0], 256)]
    scores = [dot(k_ref[at], queries, by_rows) * gain for at in chunks]
    peaks = jnp.max(functools.reduce(jnp.maximum, scores), axis=0, keepdims=True)
    weights = [jnp.exp(s - peaks) for s in scores]
    totals = jnp.sum(sum(weights), axis=0, keepdims=True)
    weights = jnp.concatenate([w.astype(jnp.bfloat16) for w in weights], axis=0)

    slots = half // unit
    odd = [n.bit_count() % 2 for n in range(slots)]

    def rows(block, other_core):
        starts = [block * count + (n + slots * (other_core ^ o)) * unit for n, o in enumerate(odd)]
        return [(lo, lo + unit) for lo in starts]

    share = 1 / totals
    votes = dot(lt_ref[...], weights, by_columns) * share
    spare = jnp.ones((out_refs[0].shape[1] - classes, 4 * count), jnp.float32)
    averages = tiles(jnp.concatenate([votes, spare], axis=0).T)
    parts = ((peaks + jnp.log(totals)).T, averages)
    far_send, near_send, far_keep, near_keep = out_refs
    encode(far_send, 0, rows_of(parts, *rows(3, 0), *rows(3, 1)), classes)
    encode(near_send, 0, rows_of(parts, *rows(0, 1), *rows(1, 0)), classes)
    keep(far_keep, 0, rows_of(parts, *rows(2, 0), *rows(2, 1)), classes)
    keep(near_keep, 0, rows_of(parts, *rows(0, 0), *rows(1, 1)), classes)


def stats(blocks, keys, labels_t, unit):
    rows, width = 4 * blocks[0].shape[0], keys.shape[1]
    bank, classes = keys.shape[0], labels_t.shape[0]
    outs = [record_shape(rows // 4, classes, d) for d in (jnp.bfloat16, jnp.float32) for _ in range(2)]
    scores = jax.ShapeDtypeStruct((rows, bank), jnp.float32)
    cost = pl.CostEstimate(
        flops=2 * rows * bank * (width + classes),
        bytes_accessed=2 * bank * (width + classes),
        transcendentals=rows * bank,
    )
    return call(
        functools.partial(stats_kernel, unit), outs, *blocks, keys, labels_t, scratch=(scores,), cost=cost
    )


def merge_kernel(put, classes, first, last, mine_ref, other_ref, *out_refs):
    half = mine_ref.shape[0] // 2
    ranges = [(at + first * half // 2, at + last * half // 2) for at in (0, half)]
    mine, other = mine_ref[...], other_ref[...].astype(jnp.float32)

    def merged(ranges):
        a, b = (jnp.concatenate([x[lo:hi] for lo, hi in ranges], axis=0) for x in (mine, other))
        return combine(kept(a, classes), decoded(b, classes))

    for p, ref, chosen in zip(put, out_refs, [[r] for r in ranges] if len(put) > 1 else [ranges]):
        p(ref, 0, merged(chosen), classes)


def merge(mine, other, classes, first, last, *put):
    rows = mine.shape[0] * (last - first) // 2 // len(put)
    outs = [record_shape(rows, classes, jnp.float32 if p is keep else jnp.bfloat16) for p in put]
    kernel = functools.partial(merge_kernel, put, classes, first, last)
    return call(kernel, outs, mine, other)


def tail_kernel(a_ref, out_ref):
    out_ref[...] = a_ref[...].astype(jnp.float32)[out_ref.shape[0] :].astype(out_ref.dtype)


def tail(a):
    out = jax.ShapeDtypeStruct((a.shape[0] // 2, a.shape[1]), a.dtype)
    return call(tail_kernel, out, a)


def finish_kernel(classes, own_ref, near_ref, far_ref, across_ref, out_ref):
    rows = out_ref.shape[0]
    came = [r[...].astype(jnp.float32)[:rows] for r in (near_ref, far_ref, across_ref)]
    _, averages = combine(kept(own_ref[...], classes), *[decoded(r, classes) for r in came])
    out_ref[...] = jnp.concatenate([jnp.log(x) for x in averages], axis=1)[:, :classes]


def finish(own, near, far, across, classes):
    out = jax.ShapeDtypeStruct((own.shape[0], classes), jnp.float32)
    return call(functools.partial(finish_kernel, classes), out, own, near, far, across)


def local(size, core, lead, queries, bank_keys, bank_labels):
    def swap(block, bit):
        return lax.ppermute(block, AXES, [(i, i ^ bit) for i in range(size)])

    def swap_far(block):
        def partner(i):
            inner = (i ^ i >> 1) & 1
            return i ^ 3 if bool(i & core) != bool(inner) else i ^ 2 ^ core

        return lax.ppermute(block, AXES, [(i, partner(i)) for i in range(size)])

    classes = bank_labels.shape[1]
    first, *rest = [bit ^ core for bit in lead] + [core]
    own = join(fetch(queries), swap(queries, first))
    for bit in rest:
        own = join(own, swap(own, bit))
    far = swap_far(own)
    near = swap(own, 1 ^ core)
    across = swap(far, core)
    *sends, far, near = stats((own, near, far, across), bank_keys, bank_labels.T, queries.shape[0])
    far_came, near_came = (swap(send, core) for send in sends)
    for bit in lead[::-1]:
        (send,) = merge(far, far_came, classes, 1, 2, encode)
        (far,) = merge(far, far_came, classes, 0, 1, keep)
        far_came = swap(send, bit)
        (send,) = merge(near, near_came, classes, 1, 2, encode)
        (near,) = merge(near, near_came, classes, 0, 1, keep)
        near_came = swap(send, bit)
    (far,) = merge(far, far_came, classes, 0, 2, encode)
    own, near = merge(near, near_came, classes, 0, 2, keep, encode)
    far = swap_far(far)
    near = swap(near, 1)
    across = swap(tail(far), core)
    return finish(own, near, far, across, classes)


def solution(mesh):
    placed = P(("groups", "bank", "query"), None)
    query, bank = mesh.shape["query"], mesh.shape["bank"]
    lead = [1 << b for b in range(2, query.bit_length() - 1)]
    lead += [query << b for b in range(1, bank.bit_length() - 1)]
    return jax.shard_map(
        functools.partial(local, query * bank, query, lead),
        mesh=mesh,
        in_specs=(placed,) * 3,
        out_specs=placed,
        check_vma=False,
    )
```

```python
import functools
import math

import jax
import jax.numpy as jnp
from jax import lax
from jax.experimental import pallas as pl
from jax.experimental.pallas import tpu as pltpu
from jax.sharding import PartitionSpec as P

SCORE_GAIN = 3.0
AXES = ("bank", "query")
LANES = 128
POWER, CENTRE = 24.0, 5.0
MIB = 1 << 20
VMEM = pl.BlockSpec(memory_space=pltpu.VMEM)
BESIDE = pl.CostEstimate(flops=4_000_000_000, bytes_accessed=1 << 17, transcendentals=0)


def grant(*arrays):
    return pltpu.CompilerParams(
        vmem_limit_bytes=sum(2 * math.prod(a.shape) * a.dtype.itemsize for a in arrays) + MIB
    )


def call(kernel, outs, *args, scratch=(), cost=None):
    return pl.pallas_call(
        kernel,
        out_shape=outs,
        in_specs=[VMEM] * len(args),
        out_specs=jax.tree.map(lambda _: VMEM, outs),
        compiler_params=grant(*args, *jax.tree.leaves(outs), *scratch),
        cost_estimate=cost,
    )(*args)


def fetch_kernel(a_ref, out_ref):
    out_ref[...] = a_ref[...]


def fetch(a):
    return call(fetch_kernel, jax.ShapeDtypeStruct(a.shape, a.dtype), a, cost=BESIDE)


def join_kernel(a_ref, b_ref, out_ref):
    both = jnp.concatenate([r[...].astype(jnp.float32) for r in (a_ref, b_ref)], axis=0)
    out_ref[...] = both.astype(out_ref.dtype)


def join(a, b):
    out = jax.ShapeDtypeStruct((2 * a.shape[0], a.shape[1]), a.dtype)
    return call(join_kernel, out, a, b, cost=BESIDE)


def record_shape(rows, classes, dtype=jnp.float32):
    return jax.ShapeDtypeStruct((rows, -(-(classes + 3) // LANES) * LANES), dtype)


def extra_columns(shape, classes, count):
    column = lax.broadcasted_iota(jnp.int32, (shape[0], LANES), 1) + (shape[1] - LANES)
    return [column == classes + c for c in range(count)]


def tiles(record):
    return [record[:, lo : lo + LANES] for lo in range(0, record.shape[1], LANES)]


def log_weight(last, shape, classes, count):
    held = functools.reduce(jnp.logical_or, extra_columns(shape, classes, count))
    return jnp.sum(jnp.where(held, last, 0.0), axis=1, keepdims=True)


def kept(record, classes):
    averages = tiles(record)
    return log_weight(averages[-1], record.shape, classes, 1), averages


def decoded(record, classes):
    codes = tiles(record)
    averages = [jnp.exp2(jnp.log2(c) * (1 / POWER) - CENTRE) for c in codes]
    return log_weight(codes[-1], record.shape, classes, 3), averages


def store(ref, at, averages, classes, extra):
    width = ref.shape[1]
    rows = averages[0].shape[0]
    for lo, values in zip(range(0, width, LANES), averages):
        if lo + LANES == width:
            for held, value in zip(extra_columns((rows, width), classes, len(extra)), extra):
                values = jnp.where(held, value, values)
        ref[at : at + rows, lo : lo + LANES] = values.astype(ref.dtype)


def keep(ref, at, parts, classes):
    store(ref, at, parts[1], classes, [parts[0]])


def encode(ref, at, parts, classes):
    log, averages = parts
    high = log.astype(jnp.bfloat16).astype(jnp.float32)
    middle = (log - high).astype(jnp.bfloat16).astype(jnp.float32)
    codes = [jnp.exp2(POWER * jnp.log2(x) + POWER * CENTRE) for x in averages]
    store(ref, at, codes, classes, [high, middle, log - high - middle])


def combine(*parts):
    top = functools.reduce(jnp.maximum, [log for log, _ in parts])
    weights = [jnp.exp(log - top) for log, _ in parts]
    total = functools.reduce(jnp.add, weights)
    factors = [w / total for w in weights]
    columns = zip(*[averages for _, averages in parts])
    return top + jnp.log(total), [sum(f * x for f, x in zip(factors, c)) for c in columns]


def rows_of(parts, *ranges):
    take = lambda x: jnp.concatenate([x[lo:hi] for lo, hi in ranges], axis=0)
    return take(parts[0]), [take(x) for x in parts[1]]


def stats_kernel(places, unit, *refs):
    *block_refs, k_ref, lt_ref = refs[:-4]
    out_refs = refs[-4:]
    width, classes = k_ref.shape[1], lt_ref.shape[0]
    queries = jnp.concatenate([r[...] for r in block_refs], axis=0)
    gain = SCORE_GAIN / math.sqrt(width)
    dot = functools.partial(lax.dot_general, preferred_element_type=jnp.float32)
    by_rows, by_columns = (((1,), (1,)), ((), ())), (((1,), (0,)), ((), ()))
    chunks = [slice(lo, lo + 256) for lo in range(0, k_ref.shape[0], 256)]
    scores = [dot(k_ref[at], queries, by_rows) * gain for at in chunks]
    peaks = jnp.max(functools.reduce(jnp.maximum, scores), axis=0, keepdims=True)
    weights = [jnp.exp(s - peaks) for s in scores]
    totals = jnp.sum(sum(weights), axis=0, keepdims=True)
    weights = jnp.concatenate([w.astype(jnp.bfloat16) for w in weights], axis=0)

    share = 1 / totals
    votes = dot(lt_ref[...], weights, by_columns) * share
    spare = jnp.ones((out_refs[0].shape[1] - classes, queries.shape[0]), jnp.float32)
    averages = tiles(jnp.concatenate([votes, spare], axis=0).T)
    parts = ((peaks + jnp.log(totals)).T, averages)
    for put, ref, chosen in zip((encode, encode, keep, keep), out_refs, places):
        put(ref, 0, rows_of(parts, *[(lo * unit, (lo + 1) * unit) for lo in chosen]), classes)


def stats(blocks, keys, labels_t, places, unit):
    rows, width = sum(b.shape[0] for b in blocks), keys.shape[1]
    bank, classes = keys.shape[0], labels_t.shape[0]
    outs = [record_shape(rows // 4, classes, d) for d in (jnp.bfloat16, jnp.float32) for _ in range(2)]
    scores = jax.ShapeDtypeStruct((rows, bank), jnp.float32)
    cost = pl.CostEstimate(
        flops=2 * rows * bank * (width + classes),
        bytes_accessed=2 * bank * (width + classes),
        transcendentals=rows * bank,
    )
    return call(
        functools.partial(stats_kernel, places, unit), outs, *blocks, keys, labels_t, scratch=(scores,), cost=cost
    )


def merge_kernel(put, classes, first, last, mine_ref, other_ref, *out_refs):
    half = mine_ref.shape[0] // 2
    ranges = [(at + first * half // 2, at + last * half // 2) for at in (0, half)]
    mine, other = mine_ref[...], other_ref[...].astype(jnp.float32)

    def merged(ranges):
        a, b = (jnp.concatenate([x[lo:hi] for lo, hi in ranges], axis=0) for x in (mine, other))
        return combine(kept(a, classes), decoded(b, classes))

    for p, ref, chosen in zip(put, out_refs, [[r] for r in ranges] if len(put) > 1 else [ranges]):
        p(ref, 0, merged(chosen), classes)


def merge(mine, other, classes, first, last, *put):
    rows = mine.shape[0] * (last - first) // 2 // len(put)
    outs = [record_shape(rows, classes, jnp.float32 if p is keep else jnp.bfloat16) for p in put]
    kernel = functools.partial(merge_kernel, put, classes, first, last)
    return call(kernel, outs, mine, other)


def tail_kernel(a_ref, out_ref):
    out_ref[...] = a_ref[...].astype(jnp.float32)[out_ref.shape[0] :].astype(out_ref.dtype)


def tail(a):
    out = jax.ShapeDtypeStruct((a.shape[0] // 2, a.shape[1]), a.dtype)
    return call(tail_kernel, out, a)


def finish_kernel(classes, own_ref, near_ref, far_ref, across_ref, out_ref):
    rows = out_ref.shape[0]
    came = [r[...].astype(jnp.float32)[:rows] for r in (near_ref, far_ref, across_ref)]
    _, averages = combine(kept(own_ref[...], classes), *[decoded(r, classes) for r in came])
    out_ref[...] = jnp.concatenate([jnp.log(x) for x in averages], axis=1)[:, :classes]


def finish(own, near, far, across, classes):
    out = jax.ShapeDtypeStruct((own.shape[0], classes), jnp.float32)
    return call(functools.partial(finish_kernel, classes), out, own, near, far, across)


def local(size, core, lead, queries, bank_keys, bank_labels):
    def swap(block, bit):
        return lax.ppermute(block, AXES, [(i, i ^ bit) for i in range(size)])

    def swap_far(block):
        def partner(i):
            inner = (i ^ i >> 1) & 1
            return i ^ 3 if bool(i & core) != bool(inner) else i ^ 2 ^ core

        return lax.ppermute(block, AXES, [(i, partner(i)) for i in range(size)])

    classes = bank_labels.shape[1]
    last, *others = lead
    masks, own, mine = [0], queries, fetch(queries)
    for bit in [bit ^ core for bit in others] + [core]:
        own = mine = join(mine, swap(own, bit))
        masks += [m ^ bit for m in masks]
    far = swap_far(own)
    near = swap(own, 1)
    across = swap(far, core)
    one = swap(join(own, far), last ^ core)
    two = swap(join(near, across), last ^ core)

    def place(first, second, flip):
        at = {m: first * len(masks) + k for k, m in enumerate(masks)}
        at |= {m ^ last ^ flip: second * len(masks) + k for k, m in enumerate(masks)}
        offsets = [0]
        for bit in lead:
            offsets += [m ^ bit for m in offsets]
        return [[at[m ^ f] for m in offsets] for f in (0, core)]

    own_rows, near_rows = place(0, 4, core), place(1, 6, core)
    far_rows, across_rows = place(2, 7, 0), place(3, 5, 0)
    odd = [n.bit_count() % 2 for n in range(1 << len(lead))]
    far_block, across_block = (far_rows, across_rows), (across_rows, far_rows)
    places = (
        [across_block[o][f][n] for f in (0, 1) for n, o in enumerate(odd)],
        [block[1 - o][n] for block in (own_rows, near_rows) for n, o in enumerate(odd)],
        [far_block[o][f][n] for f in (0, 1) for n, o in enumerate(odd)],
        [block[o][n] for block in (own_rows, near_rows) for n, o in enumerate(odd)],
    )
    blocks = (own, near, far, across, one, two)
    *sends, far, near = stats(blocks, bank_keys, bank_labels.T, places, queries.shape[0])
    far_came, near_came = (swap(send, core) for send in sends)
    for bit in lead[::-1]:
        (send,) = merge(far, far_came, classes, 1, 2, encode)
        (far,) = merge(far, far_came, classes, 0, 1, keep)
        far_came = swap(send, bit ^ core)
        (send,) = merge(near, near_came, classes, 1, 2, encode)
        (near,) = merge(near, near_came, classes, 0, 1, keep)
        near_came = swap(send, bit ^ core)
    (far,) = merge(far, far_came, classes, 0, 2, encode)
    own, near = merge(near, near_came, classes, 0, 2, keep, encode)
    far = swap_far(far)
    near = swap(near, 1)
    across = swap(tail(far), core)
    return finish(own, near, far, across, classes)


def solution(mesh):
    placed = P(("groups", "bank", "query"), None)
    query, bank = mesh.shape["query"], mesh.shape["bank"]
    lead = [1 << b for b in range(2, query.bit_length() - 1)]
    lead += [query << b for b in range(1, bank.bit_length() - 1)]
    return jax.shard_map(
        functools.partial(local, query * bank, query, lead),
        mesh=mesh,
        in_specs=(placed,) * 3,
        out_specs=placed,
        check_vma=False,
    )
```

```python
import functools
import math

import jax
import jax.numpy as jnp
from jax import lax
from jax.experimental import pallas as pl
from jax.experimental.pallas import tpu as pltpu
from jax.sharding import PartitionSpec as P

SCORE_GAIN = 3.0
AXES = ("bank", "query")
LANES = 128
POWER, CENTRE = 24.0, 5.0
MIB = 1 << 20
VMEM = pl.BlockSpec(memory_space=pltpu.VMEM)
BESIDE = pl.CostEstimate(flops=4_000_000_000, bytes_accessed=1 << 17, transcendentals=0)


def grant(*arrays):
    return pltpu.CompilerParams(
        vmem_limit_bytes=sum(2 * math.prod(a.shape) * a.dtype.itemsize for a in arrays) + MIB
    )


def call(kernel, outs, *args, scratch=(), cost=None):
    return pl.pallas_call(
        kernel,
        out_shape=outs,
        in_specs=[VMEM] * len(args),
        out_specs=jax.tree.map(lambda _: VMEM, outs),
        compiler_params=grant(*args, *jax.tree.leaves(outs), *scratch),
        cost_estimate=cost,
    )(*args)


def fetch_kernel(a_ref, out_ref):
    out_ref[...] = a_ref[...]


def fetch(a):
    return call(fetch_kernel, jax.ShapeDtypeStruct(a.shape, a.dtype), a, cost=BESIDE)


def join_kernel(a_ref, b_ref, out_ref):
    both = jnp.concatenate([r[...].astype(jnp.float32) for r in (a_ref, b_ref)], axis=0)
    out_ref[...] = both.astype(out_ref.dtype)


def join(a, b):
    out = jax.ShapeDtypeStruct((2 * a.shape[0], a.shape[1]), a.dtype)
    return call(join_kernel, out, a, b, cost=BESIDE)


def record_shape(rows, classes, dtype=jnp.float32):
    return jax.ShapeDtypeStruct((rows, -(-(classes + 3) // LANES) * LANES), dtype)


def extra_columns(shape, classes, count):
    column = lax.broadcasted_iota(jnp.int32, (shape[0], LANES), 1) + (shape[1] - LANES)
    return [column == classes + c for c in range(count)]


def tiles(record):
    return [record[:, lo : lo + LANES] for lo in range(0, record.shape[1], LANES)]


def log_weight(last, shape, classes, count):
    held = functools.reduce(jnp.logical_or, extra_columns(shape, classes, count))
    return jnp.sum(jnp.where(held, last, 0.0), axis=1, keepdims=True)


def kept(record, classes):
    averages = tiles(record)
    return log_weight(averages[-1], record.shape, classes, 1), averages


def decoded(record, classes):
    codes = tiles(record)
    averages = [jnp.exp2(jnp.log2(c) * (1 / POWER) - CENTRE) for c in codes]
    return log_weight(codes[-1], record.shape, classes, 3), averages


def store(ref, at, averages, classes, extra):
    width = ref.shape[1]
    rows = averages[0].shape[0]
    for lo, values in zip(range(0, width, LANES), averages):
        if lo + LANES == width:
            for held, value in zip(extra_columns((rows, width), classes, len(extra)), extra):
                values = jnp.where(held, value, values)
        ref[at : at + rows, lo : lo + LANES] = values.astype(ref.dtype)


def keep(ref, at, parts, classes):
    store(ref, at, parts[1], classes, [parts[0]])


def encode(ref, at, parts, classes):
    log, averages = parts
    high = log.astype(jnp.bfloat16).astype(jnp.float32)
    middle = (log - high).astype(jnp.bfloat16).astype(jnp.float32)
    codes = [jnp.exp2(POWER * jnp.log2(x) + POWER * CENTRE) for x in averages]
    store(ref, at, codes, classes, [high, middle, log - high - middle])


def combine(*parts):
    top = functools.reduce(jnp.maximum, [log for log, _ in parts])
    weights = [jnp.exp2(log - top) for log, _ in parts]
    total = functools.reduce(jnp.add, weights)
    share = 1 / total
    factors = [w * share for w in weights]
    columns = zip(*[averages for _, averages in parts])
    return top + jnp.log2(total), [sum(f * x for f, x in zip(factors, c)) for c in columns]


def rows_of(parts, *ranges):
    take = lambda x: jnp.concatenate([x[lo:hi] for lo, hi in ranges], axis=0)
    return take(parts[0]), [take(x) for x in parts[1]]


def stats_kernel(places, unit, *refs):
    *block_refs, k_ref, lt_ref = refs[:-4]
    out_refs = refs[-4:]
    width, classes = k_ref.shape[1], lt_ref.shape[0]
    queries = jnp.concatenate([r[...] for r in block_refs], axis=0)
    gain = SCORE_GAIN * math.log2(math.e) / math.sqrt(width)
    dot = functools.partial(lax.dot_general, preferred_element_type=jnp.float32)
    by_rows, by_columns = (((1,), (1,)), ((), ())), (((1,), (0,)), ((), ()))
    chunks = [slice(lo, lo + 256) for lo in range(0, k_ref.shape[0], 256)]
    scores = [dot(k_ref[at], queries, by_rows) * gain for at in chunks]
    peaks = jnp.max(functools.reduce(jnp.maximum, scores), axis=0, keepdims=True)
    weights = [jnp.exp2(s - peaks) for s in scores]
    totals = jnp.sum(sum(weights), axis=0, keepdims=True)
    weights = jnp.concatenate([w.astype(jnp.bfloat16) for w in weights], axis=0)

    share = 1 / totals
    votes = dot(lt_ref[...], weights, by_columns) * share
    spare = jnp.ones((out_refs[0].shape[1] - classes, queries.shape[0]), jnp.float32)
    averages = tiles(jnp.concatenate([votes, spare], axis=0).T)
    parts = ((peaks + jnp.log2(totals)).T, averages)
    for put, ref, chosen in zip((encode, encode, keep, keep), out_refs, places):
        put(ref, 0, rows_of(parts, *[(lo * unit, (lo + 1) * unit) for lo in chosen]), classes)


def stats(blocks, keys, labels_t, places, unit):
    rows, width = sum(b.shape[0] for b in blocks), keys.shape[1]
    bank, classes = keys.shape[0], labels_t.shape[0]
    outs = [record_shape(rows // 4, classes, d) for d in (jnp.bfloat16, jnp.float32) for _ in range(2)]
    scores = jax.ShapeDtypeStruct((rows, bank), jnp.float32)
    cost = pl.CostEstimate(
        flops=2 * rows * bank * (width + classes),
        bytes_accessed=2 * bank * (width + classes),
        transcendentals=rows * bank,
    )
    return call(
        functools.partial(stats_kernel, places, unit), outs, *blocks, keys, labels_t, scratch=(scores,), cost=cost
    )


def merge_kernel(put, classes, first, last, mine_ref, other_ref, *out_refs):
    half = mine_ref.shape[0] // 2
    ranges = [(at + first * half // 2, at + last * half // 2) for at in (0, half)]
    mine, other = mine_ref[...], other_ref[...].astype(jnp.float32)

    def merged(ranges):
        a, b = (jnp.concatenate([x[lo:hi] for lo, hi in ranges], axis=0) for x in (mine, other))
        return combine(kept(a, classes), decoded(b, classes))

    for p, ref, chosen in zip(put, out_refs, [[r] for r in ranges] if len(put) > 1 else [ranges]):
        p(ref, 0, merged(chosen), classes)


def merge(mine, other, classes, first, last, *put):
    rows = mine.shape[0] * (last - first) // 2 // len(put)
    outs = [record_shape(rows, classes, jnp.float32 if p is keep else jnp.bfloat16) for p in put]
    kernel = functools.partial(merge_kernel, put, classes, first, last)
    return call(kernel, outs, mine, other)


def tail_kernel(a_ref, out_ref):
    out_ref[...] = a_ref[...].astype(jnp.float32)[out_ref.shape[0] :].astype(out_ref.dtype)


def tail(a):
    out = jax.ShapeDtypeStruct((a.shape[0] // 2, a.shape[1]), a.dtype)
    return call(tail_kernel, out, a)


def finish_kernel(classes, own_ref, near_ref, far_ref, across_ref, out_ref):
    rows = out_ref.shape[0]
    came = [r[...].astype(jnp.float32)[:rows] for r in (near_ref, far_ref, across_ref)]
    _, averages = combine(kept(own_ref[...], classes), *[decoded(r, classes) for r in came])
    out_ref[...] = jnp.concatenate([jnp.log(x) for x in averages], axis=1)[:, :classes]


def finish(own, near, far, across, classes):
    out = jax.ShapeDtypeStruct((own.shape[0], classes), jnp.float32)
    return call(functools.partial(finish_kernel, classes), out, own, near, far, across)


def local(size, core, lead, queries, bank_keys, bank_labels):
    def swap(block, bit):
        return lax.ppermute(block, AXES, [(i, i ^ bit) for i in range(size)])

    def swap_far(block):
        def partner(i):
            inner = (i ^ i >> 1) & 1
            return i ^ 3 if bool(i & core) != bool(inner) else i ^ 2 ^ core

        return lax.ppermute(block, AXES, [(i, partner(i)) for i in range(size)])

    classes = bank_labels.shape[1]
    last, *others = lead
    masks, own, mine = [0], queries, fetch(queries)
    for bit in [bit ^ core for bit in others] + [core]:
        own = mine = join(mine, swap(own, bit))
        masks += [m ^ bit for m in masks]
    far = swap_far(own)
    near = swap(own, 1)
    across = swap(far, core)
    one = swap(join(own, far), last ^ core)
    two = swap(join(near, across), last ^ core)

    def place(first, second, flip):
        at = {m: first * len(masks) + k for k, m in enumerate(masks)}
        at |= {m ^ last ^ flip: second * len(masks) + k for k, m in enumerate(masks)}
        offsets = [0]
        for bit in lead:
            offsets += [m ^ bit for m in offsets]
        return [[at[m ^ f] for m in offsets] for f in (0, core)]

    own_rows, near_rows = place(0, 4, core), place(1, 6, core)
    far_rows, across_rows = place(2, 7, 0), place(3, 5, 0)
    odd = [n.bit_count() % 2 for n in range(1 << len(lead))]
    far_block, across_block = (far_rows, across_rows), (across_rows, far_rows)
    places = (
        [across_block[o][f][n] for f in (0, 1) for n, o in enumerate(odd)],
        [block[1 - o][n] for block in (own_rows, near_rows) for n, o in enumerate(odd)],
        [far_block[o][f][n] for f in (0, 1) for n, o in enumerate(odd)],
        [block[o][n] for block in (own_rows, near_rows) for n, o in enumerate(odd)],
    )
    blocks = (own, near, far, across, one, two)
    *sends, far, near = stats(blocks, bank_keys, bank_labels.T, places, queries.shape[0])
    far_came, near_came = (swap(send, core) for send in sends)
    for bit in lead[::-1]:
        (send,) = merge(far, far_came, classes, 1, 2, encode)
        (far,) = merge(far, far_came, classes, 0, 1, keep)
        far_came = swap(send, bit ^ core)
        (send,) = merge(near, near_came, classes, 1, 2, encode)
        (near,) = merge(near, near_came, classes, 0, 1, keep)
        near_came = swap(send, bit ^ core)
    (far,) = merge(far, far_came, classes, 0, 2, encode)
    own, near = merge(near, near_came, classes, 0, 2, keep, encode)
    far = swap_far(far)
    near = swap(near, 1)
    across = swap(tail(far), core)
    return finish(own, near, far, across, classes)


def solution(mesh):
    placed = P(("groups", "bank", "query"), None)
    query, bank = mesh.shape["query"], mesh.shape["bank"]
    lead = [1 << b for b in range(2, query.bit_length() - 1)]
    lead += [query << b for b in range(1, bank.bit_length() - 1)]
    return jax.shard_map(
        functools.partial(local, query * bank, query, lead),
        mesh=mesh,
        in_specs=(placed,) * 3,
        out_specs=placed,
        check_vma=False,
    )
```

```python
import functools
import math

import jax
import jax.numpy as jnp
from jax import lax
from jax.experimental import pallas as pl
from jax.experimental.pallas import tpu as pltpu
from jax.sharding import PartitionSpec as P

SCORE_GAIN = 3.0
AXES = ("bank", "query")
LANES = 128
POWER, CENTRE = 24.0, 5.0
MIB = 1 << 20
VMEM = pl.BlockSpec(memory_space=pltpu.VMEM)
BESIDE = pl.CostEstimate(flops=4_000_000_000, bytes_accessed=1 << 17, transcendentals=0)


def grant(*arrays):
    return pltpu.CompilerParams(
        vmem_limit_bytes=sum(2 * math.prod(a.shape) * a.dtype.itemsize for a in arrays) + MIB
    )


def call(kernel, outs, *args, scratch=(), cost=None):
    return pl.pallas_call(
        kernel,
        out_shape=outs,
        in_specs=[VMEM] * len(args),
        out_specs=jax.tree.map(lambda _: VMEM, outs),
        compiler_params=grant(*args, *jax.tree.leaves(outs), *scratch),
        cost_estimate=cost,
    )(*args)


def fetch_kernel(a_ref, out_ref):
    out_ref[...] = a_ref[...]


def fetch(a):
    return call(fetch_kernel, jax.ShapeDtypeStruct(a.shape, a.dtype), a, cost=BESIDE)


def join_kernel(a_ref, b_ref, out_ref):
    both = jnp.concatenate([r[...].astype(jnp.float32) for r in (a_ref, b_ref)], axis=0)
    out_ref[...] = both.astype(out_ref.dtype)


def join(a, b):
    out = jax.ShapeDtypeStruct((2 * a.shape[0], a.shape[1]), a.dtype)
    return call(join_kernel, out, a, b, cost=BESIDE)


def record_shape(rows, classes, dtype=jnp.float32):
    return jax.ShapeDtypeStruct((rows, -(-(classes + 3) // LANES) * LANES), dtype)


def extra_columns(shape, classes, count):
    column = lax.broadcasted_iota(jnp.int32, (shape[0], LANES), 1) + (shape[1] - LANES)
    return [column == classes + c for c in range(count)]


def tiles(record):
    return [record[:, lo : lo + LANES] for lo in range(0, record.shape[1], LANES)]


def log_weight(last, shape, classes, count):
    held = functools.reduce(jnp.logical_or, extra_columns(shape, classes, count))
    return jnp.sum(jnp.where(held, last, 0.0), axis=1, keepdims=True)


def kept(record, classes):
    averages = tiles(record)
    return log_weight(averages[-1], record.shape, classes, 1), averages


def decoded(record, classes):
    codes = tiles(record)
    averages = [jnp.exp2(jnp.log2(c) * (1 / POWER) - CENTRE) for c in codes]
    return log_weight(codes[-1], record.shape, classes, 3), averages


def store(ref, at, averages, classes, extra):
    width = ref.shape[1]
    rows = averages[0].shape[0]
    for lo, values in zip(range(0, width, LANES), averages):
        if lo + LANES == width:
            for held, value in zip(extra_columns((rows, width), classes, len(extra)), extra):
                values = jnp.where(held, value, values)
        ref[at : at + rows, lo : lo + LANES] = values.astype(ref.dtype)


def keep(ref, at, parts, classes):
    store(ref, at, parts[1], classes, [parts[0]])


def encode(ref, at, parts, classes):
    log, averages = parts
    high = log.astype(jnp.bfloat16).astype(jnp.float32)
    middle = (log - high).astype(jnp.bfloat16).astype(jnp.float32)
    codes = [jnp.exp2(POWER * jnp.log2(x) + POWER * CENTRE) for x in averages]
    store(ref, at, codes, classes, [high, middle, log - high - middle])


def combine(*parts):
    top = functools.reduce(jnp.maximum, [log for log, _ in parts])
    weights = [jnp.exp2(log - top) for log, _ in parts]
    total = functools.reduce(jnp.add, weights)
    share = 1 / total
    factors = [w * share for w in weights]
    columns = zip(*[averages for _, averages in parts])
    return top + jnp.log2(total), [sum(f * x for f, x in zip(factors, c)) for c in columns]


def rows_of(parts, *ranges):
    take = lambda x: jnp.concatenate([x[lo:hi] for lo, hi in ranges], axis=0)
    return take(parts[0]), [take(x) for x in parts[1]]


def stats_kernel(places, unit, *refs):
    *block_refs, k_ref, lt_ref = refs[:-4]
    out_refs = refs[-4:]
    width, classes = k_ref.shape[1], lt_ref.shape[0]
    queries = jnp.concatenate([r[...] for r in block_refs], axis=0)
    gain = SCORE_GAIN * math.log2(math.e) / math.sqrt(width)
    dot = functools.partial(lax.dot_general, preferred_element_type=jnp.float32)
    by_rows, by_columns = (((1,), (1,)), ((), ())), (((1,), (0,)), ((), ()))
    chunks = [slice(lo, lo + 256) for lo in range(0, k_ref.shape[0], 256)]
    scores = [dot(k_ref[at], queries, by_rows) * gain for at in chunks]
    peaks = jnp.max(functools.reduce(jnp.maximum, scores), axis=0, keepdims=True)
    weights = [jnp.exp2(s - peaks) for s in scores]
    totals = jnp.sum(sum(weights), axis=0, keepdims=True)
    weights = jnp.concatenate([w.astype(jnp.bfloat16) for w in weights], axis=0)

    share = 1 / totals
    votes = dot(lt_ref[...], weights, by_columns) * share
    spare = jnp.ones((out_refs[0].shape[1] - classes, queries.shape[0]), jnp.float32)
    averages = tiles(jnp.concatenate([votes, spare], axis=0).T)
    parts = ((peaks + jnp.log2(totals)).T, averages)
    for put, ref, chosen in zip((encode, encode, keep, keep), out_refs, places):
        put(ref, 0, rows_of(parts, *[(lo * unit, (lo + 1) * unit) for lo in chosen]), classes)


def stats(blocks, keys, labels_t, places, unit):
    rows, width = sum(b.shape[0] for b in blocks), keys.shape[1]
    bank, classes = keys.shape[0], labels_t.shape[0]
    outs = [record_shape(rows // 4, classes, d) for d in (jnp.bfloat16, jnp.float32) for _ in range(2)]
    scores = jax.ShapeDtypeStruct((rows, bank), jnp.float32)
    cost = pl.CostEstimate(
        flops=2 * rows * bank * (width + classes),
        bytes_accessed=2 * bank * (width + classes),
        transcendentals=rows * bank,
    )
    return call(
        functools.partial(stats_kernel, places, unit), outs, *blocks, keys, labels_t, scratch=(scores,), cost=cost
    )


def merge_kernel(put, classes, first, last, mine_ref, other_ref, *out_refs):
    half = mine_ref.shape[0] // 2
    ranges = [(at + first * half // 2, at + last * half // 2) for at in (0, half)]
    mine, other = mine_ref[...], other_ref[...].astype(jnp.float32)

    def merged(ranges):
        a, b = (jnp.concatenate([x[lo:hi] for lo, hi in ranges], axis=0) for x in (mine, other))
        return combine(kept(a, classes), decoded(b, classes))

    for p, ref, chosen in zip(put, out_refs, [[r] for r in ranges] if len(put) > 1 else [ranges]):
        p(ref, 0, merged(chosen), classes)


def merge(mine, other, classes, first, last, *put):
    rows = mine.shape[0] * (last - first) // 2 // len(put)
    outs = [record_shape(rows, classes, jnp.float32 if p is keep else jnp.bfloat16) for p in put]
    kernel = functools.partial(merge_kernel, put, classes, first, last)
    return call(kernel, outs, mine, other)


def tail_kernel(a_ref, out_ref):
    out_ref[...] = a_ref[...].astype(jnp.float32)[out_ref.shape[0] :].astype(out_ref.dtype)


def tail(a):
    out = jax.ShapeDtypeStruct((a.shape[0] // 2, a.shape[1]), a.dtype)
    return call(tail_kernel, out, a)


def add_kernel(classes, own_ref, far_ref, out_ref):
    far = far_ref[...].astype(jnp.float32)[: own_ref.shape[0]]
    keep(out_ref, 0, combine(kept(own_ref[...], classes), decoded(far, classes)), classes)


def add(own, far, classes):
    out = record_shape(own.shape[0], classes)
    return call(functools.partial(add_kernel, classes), out, own, far)


def finish_kernel(classes, own_ref, near_ref, across_ref, out_ref):
    came = [decoded(r[...].astype(jnp.float32), classes) for r in (near_ref, across_ref)]
    _, averages = combine(kept(own_ref[...], classes), *came)
    out_ref[...] = jnp.concatenate([jnp.log(x) for x in averages], axis=1)[:, :classes]


def finish(own, near, across, classes):
    out = jax.ShapeDtypeStruct((own.shape[0], classes), jnp.float32)
    return call(functools.partial(finish_kernel, classes), out, own, near, across)


def local(size, core, lead, queries, bank_keys, bank_labels):
    def swap(block, bit):
        return lax.ppermute(block, AXES, [(i, i ^ bit) for i in range(size)])

    def swap_far(block):
        def partner(i):
            inner = (i ^ i >> 1) & 1
            return i ^ 3 if bool(i & core) != bool(inner) else i ^ 2 ^ core

        return lax.ppermute(block, AXES, [(i, partner(i)) for i in range(size)])

    classes = bank_labels.shape[1]
    last, *others = lead
    masks, own, mine = [0], queries, fetch(queries)
    for bit in [bit ^ core for bit in others] + [core]:
        own = mine = join(mine, swap(own, bit))
        masks += [m ^ bit for m in masks]
    far = swap_far(own)
    near = swap(own, 1)
    across = swap(far, core)
    one = swap(join(own, far), last ^ core)
    two = swap(join(near, across), last ^ core)

    def place(first, second, flip):
        at = {m: first * len(masks) + k for k, m in enumerate(masks)}
        at |= {m ^ last ^ flip: second * len(masks) + k for k, m in enumerate(masks)}
        offsets = [0]
        for bit in lead:
            offsets += [m ^ bit for m in offsets]
        return [[at[m ^ f] for m in offsets] for f in (0, core)]

    own_rows, near_rows = place(0, 4, core), place(1, 6, core)
    far_rows, across_rows = place(2, 7, 0), place(3, 5, 0)
    odd = [n.bit_count() % 2 for n in range(1 << len(lead))]
    far_block, across_block = (far_rows, across_rows), (across_rows, far_rows)
    places = (
        [across_block[o][f][n] for f in (0, 1) for n, o in enumerate(odd)],
        [block[1 - o][n] for block in (own_rows, near_rows) for n, o in enumerate(odd)],
        [far_block[o][f][n] for f in (0, 1) for n, o in enumerate(odd)],
        [block[o][n] for block in (own_rows, near_rows) for n, o in enumerate(odd)],
    )
    blocks = (own, near, far, across, one, two)
    *sends, far, near = stats(blocks, bank_keys, bank_labels.T, places, queries.shape[0])
    far_came, near_came = (swap(send, core) for send in sends)
    for bit in lead[::-1]:
        (send,) = merge(far, far_came, classes, 1, 2, encode)
        (far,) = merge(far, far_came, classes, 0, 1, keep)
        far_came = swap(send, bit ^ core)
        (send,) = merge(near, near_came, classes, 1, 2, encode)
        (near,) = merge(near, near_came, classes, 0, 1, keep)
        near_came = swap(send, bit ^ core)
    (far,) = merge(far, far_came, classes, 0, 2, encode)
    own, near = merge(near, near_came, classes, 0, 2, keep, encode)
    far = swap_far(far)
    near = swap(near, 1)
    across = swap(tail(far), core)
    return finish(add(own, far, classes), near, across, classes)


def solution(mesh):
    placed = P(("groups", "bank", "query"), None)
    query, bank = mesh.shape["query"], mesh.shape["bank"]
    lead = [1 << b for b in range(2, query.bit_length() - 1)]
    lead += [query << b for b in range(1, bank.bit_length() - 1)]
    return jax.shard_map(
        functools.partial(local, query * bank, query, lead),
        mesh=mesh,
        in_specs=(placed,) * 3,
        out_specs=placed,
        check_vma=False,
    )
```

```python
import functools
import math

import jax
import jax.numpy as jnp
from jax import lax
from jax.experimental import pallas as pl
from jax.experimental.pallas import tpu as pltpu
from jax.sharding import PartitionSpec as P

SCORE_GAIN = 3.0
AXES = ("bank", "query")
LANES = 128
POWER, CENTRE = 24.0, 5.0
MIB = 1 << 20
VMEM = pl.BlockSpec(memory_space=pltpu.VMEM)
BESIDE = pl.CostEstimate(flops=4_000_000_000, bytes_accessed=1 << 17, transcendentals=0)


def grant(*arrays):
    return pltpu.CompilerParams(
        vmem_limit_bytes=sum(2 * math.prod(a.shape) * a.dtype.itemsize for a in arrays) + MIB
    )


def call(kernel, outs, *args, scratch=(), cost=None):
    return pl.pallas_call(
        kernel,
        out_shape=outs,
        in_specs=[VMEM] * len(args),
        out_specs=jax.tree.map(lambda _: VMEM, outs),
        compiler_params=grant(*args, *jax.tree.leaves(outs), *scratch),
        cost_estimate=cost,
    )(*args)


def fetch_kernel(a_ref, out_ref):
    out_ref[...] = a_ref[...]


def fetch(a):
    return call(fetch_kernel, jax.ShapeDtypeStruct(a.shape, a.dtype), a, cost=BESIDE)


def join_kernel(a_ref, b_ref, out_ref):
    both = jnp.concatenate([r[...].astype(jnp.float32) for r in (a_ref, b_ref)], axis=0)
    out_ref[...] = both.astype(out_ref.dtype)


def join(a, b):
    out = jax.ShapeDtypeStruct((2 * a.shape[0], a.shape[1]), a.dtype)
    return call(join_kernel, out, a, b, cost=BESIDE)


def record_shape(rows, classes, dtype=jnp.float32):
    return jax.ShapeDtypeStruct((rows, -(-(classes + 3) // LANES) * LANES), dtype)


def extra_columns(shape, classes, count):
    column = lax.broadcasted_iota(jnp.int32, (shape[0], LANES), 1) + (shape[1] - LANES)
    return [column == classes + c for c in range(count)]


def tiles(record):
    return [record[:, lo : lo + LANES] for lo in range(0, record.shape[1], LANES)]


def log_weight(last, shape, classes, count):
    held = functools.reduce(jnp.logical_or, extra_columns(shape, classes, count))
    return jnp.sum(jnp.where(held, last, 0.0), axis=1, keepdims=True)


def kept(record, classes):
    averages = tiles(record)
    return log_weight(averages[-1], record.shape, classes, 1), averages


def decoded(record, classes):
    codes = tiles(record)
    averages = [jnp.exp2(jnp.log2(c) * (1 / POWER) - CENTRE) for c in codes]
    return log_weight(codes[-1], record.shape, classes, 3), averages


def store(ref, at, averages, classes, extra):
    width = ref.shape[1]
    rows = averages[0].shape[0]
    for lo, values in zip(range(0, width, LANES), averages):
        if lo + LANES == width:
            for held, value in zip(extra_columns((rows, width), classes, len(extra)), extra):
                values = jnp.where(held, value, values)
        ref[at : at + rows, lo : lo + LANES] = values.astype(ref.dtype)


def keep(ref, at, parts, classes):
    store(ref, at, parts[1], classes, [parts[0]])


def encode(ref, at, parts, classes):
    log, averages = parts
    high = log.astype(jnp.bfloat16).astype(jnp.float32)
    middle = (log - high).astype(jnp.bfloat16).astype(jnp.float32)
    codes = [jnp.exp2(POWER * jnp.log2(x) + POWER * CENTRE) for x in averages]
    store(ref, at, codes, classes, [high, middle, log - high - middle])


def combine(*parts):
    top = functools.reduce(jnp.maximum, [log for log, _ in parts])
    weights = [jnp.exp2(log - top) for log, _ in parts]
    total = functools.reduce(jnp.add, weights)
    share = 1 / total
    factors = [w * share for w in weights]
    columns = zip(*[averages for _, averages in parts])
    return top + jnp.log2(total), [sum(f * x for f, x in zip(factors, c)) for c in columns]


def rows_of(parts, *ranges):
    take = lambda x: jnp.concatenate([x[lo:hi] for lo, hi in ranges], axis=0)
    return take(parts[0]), [take(x) for x in parts[1]]


def stats_kernel(places, unit, *refs):
    *block_refs, k_ref, lt_ref = refs[:-4]
    out_refs = refs[-4:]
    width, classes = k_ref.shape[1], lt_ref.shape[0]
    queries = jnp.concatenate([r[...] for r in block_refs], axis=0)
    gain = SCORE_GAIN * math.log2(math.e) / math.sqrt(width)
    dot = functools.partial(lax.dot_general, preferred_element_type=jnp.float32)
    by_rows, by_columns = (((1,), (1,)), ((), ())), (((1,), (0,)), ((), ()))
    chunks = [slice(lo, lo + 256) for lo in range(0, k_ref.shape[0], 256)]
    scores = [dot(k_ref[at], queries, by_rows) * gain for at in chunks]
    peaks = jnp.max(functools.reduce(jnp.maximum, scores), axis=0, keepdims=True)
    weights = [jnp.exp2(s - peaks) for s in scores]
    totals = jnp.sum(sum(weights), axis=0, keepdims=True)
    weights = jnp.concatenate([w.astype(jnp.bfloat16) for w in weights], axis=0)

    share = 1 / totals
    votes = dot(lt_ref[...], weights, by_columns) * share
    spare = jnp.ones((out_refs[0].shape[1] - classes, queries.shape[0]), jnp.float32)
    averages = tiles(jnp.concatenate([votes, spare], axis=0).T)
    parts = ((peaks + jnp.log2(totals)).T, averages)
    for put, ref, chosen in zip((encode, encode, keep, keep), out_refs, places):
        put(ref, 0, rows_of(parts, *[(lo * unit, (lo + 1) * unit) for lo in chosen]), classes)


def stats(blocks, keys, labels_t, places, unit):
    rows, width = sum(b.shape[0] for b in blocks), keys.shape[1]
    bank, classes = keys.shape[0], labels_t.shape[0]
    outs = [record_shape(rows // 4, classes, d) for d in (jnp.bfloat16, jnp.float32) for _ in range(2)]
    scores = jax.ShapeDtypeStruct((rows, bank), jnp.float32)
    cost = pl.CostEstimate(
        flops=2 * rows * bank * (width + classes),
        bytes_accessed=2 * bank * (width + classes),
        transcendentals=rows * bank,
    )
    return call(
        functools.partial(stats_kernel, places, unit), outs, *blocks, keys, labels_t, scratch=(scores,), cost=cost
    )


def merge_kernel(put, classes, first, last, mine_ref, other_ref, *out_refs):
    half = mine_ref.shape[0] // 2
    ranges = [(at + first * half // 2, at + last * half // 2) for at in (0, half)]
    mine, other = mine_ref[...], other_ref[...].astype(jnp.float32)

    def merged(ranges):
        a, b = (jnp.concatenate([x[lo:hi] for lo, hi in ranges], axis=0) for x in (mine, other))
        return combine(kept(a, classes), decoded(b, classes))

    wanted = zip(put, [[r] for r in ranges] if len(put) > 1 else [ranges])
    for (p, chosen), ref in zip([w for w in wanted if w[0] is not None], out_refs):
        p(ref, 0, merged(chosen), classes)


def merge(mine, other, classes, first, last, *put):
    rows = mine.shape[0] * (last - first) // 2 // len(put)
    forms = [p for p in put if p is not None]
    outs = [record_shape(rows, classes, jnp.float32 if p is keep else jnp.bfloat16) for p in forms]
    kernel = functools.partial(merge_kernel, put, classes, first, last)
    return call(kernel, outs, mine, other)


def tail_kernel(a_ref, out_ref):
    out_ref[...] = a_ref[...].astype(jnp.float32)[out_ref.shape[0] :].astype(out_ref.dtype)


def tail(a):
    out = jax.ShapeDtypeStruct((a.shape[0] // 2, a.shape[1]), a.dtype)
    return call(tail_kernel, out, a)


def add_kernel(classes, own_ref, far_ref, out_ref):
    far = far_ref[...].astype(jnp.float32)[: own_ref.shape[0]]
    keep(out_ref, 0, combine(kept(own_ref[...], classes), decoded(far, classes)), classes)


def add(own, far, classes):
    out = record_shape(own.shape[0], classes)
    return call(functools.partial(add_kernel, classes), out, own, far)


def finish_kernel(classes, own_ref, near_ref, across_ref, out_ref):
    came = [decoded(r[...].astype(jnp.float32), classes) for r in (near_ref, across_ref)]
    _, averages = combine(kept(own_ref[...], classes), *came)
    out_ref[...] = jnp.concatenate([jnp.log(x) for x in averages], axis=1)[:, :classes]


def finish(own, near, across, classes):
    out = jax.ShapeDtypeStruct((own.shape[0], classes), jnp.float32)
    return call(functools.partial(finish_kernel, classes), out, own, near, across)


def local(size, core, lead, queries, bank_keys, bank_labels):
    def swap(block, bit):
        return lax.ppermute(block, AXES, [(i, i ^ bit) for i in range(size)])

    def swap_far(block):
        def partner(i):
            inner = (i ^ i >> 1) & 1
            return i ^ 3 if bool(i & core) != bool(inner) else i ^ 2 ^ core

        return lax.ppermute(block, AXES, [(i, partner(i)) for i in range(size)])

    classes = bank_labels.shape[1]
    last, *others = lead
    masks, own, mine = [0], queries, fetch(queries)
    for bit in [bit ^ core for bit in others] + [core]:
        own = mine = join(mine, swap(own, bit))
        masks += [m ^ bit for m in masks]
    far = swap_far(own)
    near = swap(own, 1)
    across = swap(far, core)
    one = swap(join(own, far), last ^ core)
    two = swap(join(near, across), last ^ core)

    def place(first, second, flip):
        at = {m: first * len(masks) + k for k, m in enumerate(masks)}
        at |= {m ^ last ^ flip: second * len(masks) + k for k, m in enumerate(masks)}
        offsets = [0]
        for bit in lead:
            offsets += [m ^ bit for m in offsets]
        return [[at[m ^ f] for m in offsets] for f in (0, core)]

    own_rows, near_rows = place(0, 4, core), place(1, 6, core)
    far_rows, across_rows = place(2, 7, 0), place(3, 5, 0)
    odd = [n.bit_count() % 2 for n in range(1 << len(lead))]
    far_block, across_block = (far_rows, across_rows), (across_rows, far_rows)
    places = (
        [across_block[o][f][n] for f in (0, 1) for n, o in enumerate(odd)],
        [block[1 - o][n] for block in (own_rows, near_rows) for n, o in enumerate(odd)],
        [far_block[o][f][n] for f in (0, 1) for n, o in enumerate(odd)],
        [block[o][n] for block in (own_rows, near_rows) for n, o in enumerate(odd)],
    )
    blocks = (own, near, far, across, one, two)
    *sends, far, near = stats(blocks, bank_keys, bank_labels.T, places, queries.shape[0])
    far_came, near_came = (swap(send, core) for send in sends)
    for bit in lead[::-1]:
        (send,) = merge(far, far_came, classes, 1, 2, encode)
        (far,) = merge(far, far_came, classes, 0, 1, keep)
        far_came = swap(send, bit ^ core)
        (send,) = merge(near, near_came, classes, 1, 2, encode)
        (near,) = merge(near, near_came, classes, 0, 1, keep)
        near_came = swap(send, bit ^ core)
    (far,) = merge(far, far_came, classes, 0, 2, encode)
    (own,) = merge(near, near_came, classes, 0, 2, keep, None)
    (near,) = merge(near, near_came, classes, 0, 2, None, encode)
    far = swap_far(far)
    near = swap(near, 1)
    across = swap(tail(far), core)
    return finish(add(own, far, classes), near, across, classes)


def solution(mesh):
    placed = P(("groups", "bank", "query"), None)
    query, bank = mesh.shape["query"], mesh.shape["bank"]
    lead = [1 << b for b in range(2, query.bit_length() - 1)]
    lead += [query << b for b in range(1, bank.bit_length() - 1)]
    return jax.shard_map(
        functools.partial(local, query * bank, query, lead),
        mesh=mesh,
        in_specs=(placed,) * 3,
        out_specs=placed,
        check_vma=False,
    )
```

```python
import functools
import math

import jax
import jax.numpy as jnp
from jax import lax
from jax.experimental import pallas as pl
from jax.experimental.pallas import tpu as pltpu
from jax.sharding import PartitionSpec as P

SCORE_GAIN = 3.0
AXES = ("bank", "query")
LANES = 128
POWER, CENTRE = 24.0, 5.0
MIB = 1 << 20
VMEM = pl.BlockSpec(memory_space=pltpu.VMEM)
BESIDE = pl.CostEstimate(flops=4_000_000_000, bytes_accessed=1 << 17, transcendentals=0)


def grant(*arrays):
    return pltpu.CompilerParams(
        vmem_limit_bytes=sum(2 * math.prod(a.shape) * a.dtype.itemsize for a in arrays) + MIB
    )


def call(kernel, outs, *args, scratch=(), cost=None):
    return pl.pallas_call(
        kernel,
        out_shape=outs,
        in_specs=[VMEM] * len(args),
        out_specs=jax.tree.map(lambda _: VMEM, outs),
        compiler_params=grant(*args, *jax.tree.leaves(outs), *scratch),
        cost_estimate=cost,
    )(*args)


def fetch_kernel(a_ref, out_ref):
    out_ref[...] = a_ref[...]


def fetch(a):
    return call(fetch_kernel, jax.ShapeDtypeStruct(a.shape, a.dtype), a, cost=BESIDE)


def join_kernel(a_ref, b_ref, out_ref):
    both = jnp.concatenate([r[...].astype(jnp.float32) for r in (a_ref, b_ref)], axis=0)
    out_ref[...] = both.astype(out_ref.dtype)


def join(a, b):
    out = jax.ShapeDtypeStruct((2 * a.shape[0], a.shape[1]), a.dtype)
    return call(join_kernel, out, a, b, cost=BESIDE)


def record_shape(rows, classes, dtype=jnp.float32):
    return jax.ShapeDtypeStruct((rows, -(-(classes + 3) // LANES) * LANES), dtype)


def extra_columns(shape, classes, count):
    column = lax.broadcasted_iota(jnp.int32, (shape[0], LANES), 1) + (shape[1] - LANES)
    return [column == classes + c for c in range(count)]


def tiles(record):
    return [record[:, lo : lo + LANES] for lo in range(0, record.shape[1], LANES)]


def log_weight(last, shape, classes, count):
    held = functools.reduce(jnp.logical_or, extra_columns(shape, classes, count))
    return jnp.sum(jnp.where(held, last, 0.0), axis=1, keepdims=True)


def kept(record, classes):
    averages = tiles(record)
    return log_weight(averages[-1], record.shape, classes, 1), averages


def decoded(record, classes):
    codes = tiles(record)
    averages = [jnp.exp2(jnp.log2(c) * (1 / POWER) - CENTRE) for c in codes]
    return log_weight(codes[-1], record.shape, classes, 3), averages


def store(ref, at, averages, classes, extra):
    width = ref.shape[1]
    rows = averages[0].shape[0]
    for lo, values in zip(range(0, width, LANES), averages):
        if lo + LANES == width:
            for held, value in zip(extra_columns((rows, width), classes, len(extra)), extra):
                values = jnp.where(held, value, values)
        ref[at : at + rows, lo : lo + LANES] = values.astype(ref.dtype)


def keep(ref, at, parts, classes):
    store(ref, at, parts[1], classes, [parts[0]])


def encode(ref, at, parts, classes):
    log, averages = parts
    high = log.astype(jnp.bfloat16).astype(jnp.float32)
    middle = (log - high).astype(jnp.bfloat16).astype(jnp.float32)
    codes = [jnp.exp2(POWER * jnp.log2(x) + POWER * CENTRE) for x in averages]
    store(ref, at, codes, classes, [high, middle, log - high - middle])


def combine(*parts):
    top = functools.reduce(jnp.maximum, [log for log, _ in parts])
    weights = [jnp.exp2(log - top) for log, _ in parts]
    total = functools.reduce(jnp.add, weights)
    share = 1 / total
    factors = [w * share for w in weights]
    columns = zip(*[averages for _, averages in parts])
    return top + jnp.log2(total), [sum(f * x for f, x in zip(factors, c)) for c in columns]


def rows_of(parts, *ranges):
    take = lambda x: jnp.concatenate([x[lo:hi] for lo, hi in ranges], axis=0)
    return take(parts[0]), [take(x) for x in parts[1]]


def stats_kernel(places, unit, *refs):
    *block_refs, k_ref, lt_ref = refs[:-4]
    out_refs = refs[-4:]
    width, classes = k_ref.shape[1], lt_ref.shape[0]
    queries = jnp.concatenate([r[...] for r in block_refs], axis=0)
    gain = SCORE_GAIN * math.log2(math.e) / math.sqrt(width)
    dot = functools.partial(lax.dot_general, preferred_element_type=jnp.float32)
    by_rows, by_columns = (((1,), (1,)), ((), ())), (((1,), (0,)), ((), ()))
    chunks = [slice(lo, lo + 512) for lo in range(0, k_ref.shape[0], 512)]
    scores = [dot(k_ref[at], queries, by_rows) * gain for at in chunks]
    peaks = jnp.max(functools.reduce(jnp.maximum, scores), axis=0, keepdims=True)
    weights = [jnp.exp2(s - peaks) for s in scores]
    totals = jnp.sum(sum(weights), axis=0, keepdims=True)
    weights = jnp.concatenate([w.astype(jnp.bfloat16) for w in weights], axis=0)

    share = 1 / totals
    votes = dot(lt_ref[...], weights, by_columns) * share
    spare = jnp.ones((out_refs[0].shape[1] - classes, queries.shape[0]), jnp.float32)
    averages = tiles(jnp.concatenate([votes, spare], axis=0).T)
    parts = ((peaks + jnp.log2(totals)).T, averages)
    for put, ref, chosen in zip((encode, encode, keep, keep), out_refs, places):
        put(ref, 0, rows_of(parts, *[(lo * unit, (lo + 1) * unit) for lo in chosen]), classes)


def stats(blocks, keys, labels_t, places, unit):
    rows, width = sum(b.shape[0] for b in blocks), keys.shape[1]
    bank, classes = keys.shape[0], labels_t.shape[0]
    outs = [record_shape(rows // 4, classes, d) for d in (jnp.bfloat16, jnp.float32) for _ in range(2)]
    scores = jax.ShapeDtypeStruct((rows, bank), jnp.float32)
    cost = pl.CostEstimate(
        flops=2 * rows * bank * (width + classes),
        bytes_accessed=2 * bank * (width + classes),
        transcendentals=rows * bank,
    )
    return call(
        functools.partial(stats_kernel, places, unit), outs, *blocks, keys, labels_t, scratch=(scores,), cost=cost
    )


def merge_kernel(put, classes, first, last, mine_ref, other_ref, *out_refs):
    half = mine_ref.shape[0] // 2
    ranges = [(at + first * half // 2, at + last * half // 2) for at in (0, half)]
    mine, other = mine_ref[...], other_ref[...].astype(jnp.float32)

    def merged(ranges):
        a, b = (jnp.concatenate([x[lo:hi] for lo, hi in ranges], axis=0) for x in (mine, other))
        return combine(kept(a, classes), decoded(b, classes))

    for p, ref, chosen in zip(put, out_refs, [[r] for r in ranges] if len(put) > 1 else [ranges]):
        p(ref, 0, merged(chosen), classes)


def merge(mine, other, classes, first, last, *put):
    rows = mine.shape[0] * (last - first) // 2 // len(put)
    outs = [record_shape(rows, classes, jnp.float32 if p is keep else jnp.bfloat16) for p in put]
    kernel = functools.partial(merge_kernel, put, classes, first, last)
    return call(kernel, outs, mine, other)


def tail_kernel(a_ref, out_ref):
    out_ref[...] = a_ref[...].astype(jnp.float32)[out_ref.shape[0] :].astype(out_ref.dtype)


def tail(a):
    out = jax.ShapeDtypeStruct((a.shape[0] // 2, a.shape[1]), a.dtype)
    return call(tail_kernel, out, a)


def add_kernel(classes, own_ref, far_ref, out_ref):
    far = far_ref[...].astype(jnp.float32)[: own_ref.shape[0]]
    keep(out_ref, 0, combine(kept(own_ref[...], classes), decoded(far, classes)), classes)


def add(own, far, classes):
    out = record_shape(own.shape[0], classes)
    return call(functools.partial(add_kernel, classes), out, own, far)


def finish_kernel(classes, own_ref, near_ref, across_ref, out_ref):
    came = [decoded(r[...].astype(jnp.float32), classes) for r in (near_ref, across_ref)]
    _, averages = combine(kept(own_ref[...], classes), *came)
    out_ref[...] = jnp.concatenate([jnp.log(x) for x in averages], axis=1)[:, :classes]


def finish(own, near, across, classes):
    out = jax.ShapeDtypeStruct((own.shape[0], classes), jnp.float32)
    return call(functools.partial(finish_kernel, classes), out, own, near, across)


def local(size, core, lead, queries, bank_keys, bank_labels):
    def swap(block, bit):
        return lax.ppermute(block, AXES, [(i, i ^ bit) for i in range(size)])

    def swap_far(block):
        def partner(i):
            inner = (i ^ i >> 1) & 1
            return i ^ 3 if bool(i & core) != bool(inner) else i ^ 2 ^ core

        return lax.ppermute(block, AXES, [(i, partner(i)) for i in range(size)])

    classes = bank_labels.shape[1]
    last, *others = lead
    masks, own, mine = [0], queries, fetch(queries)
    for bit in [bit ^ core for bit in others] + [core]:
        own = mine = join(mine, swap(own, bit))
        masks += [m ^ bit for m in masks]
    far = swap_far(own)
    near = swap(own, 1)
    across = swap(far, core)
    one = swap(join(own, far), last ^ core)
    two = swap(join(near, across), last ^ core)

    def place(first, second, flip):
        at = {m: first * len(masks) + k for k, m in enumerate(masks)}
        at |= {m ^ last ^ flip: second * len(masks) + k for k, m in enumerate(masks)}
        offsets = [0]
        for bit in lead:
            offsets += [m ^ bit for m in offsets]
        return [[at[m ^ f] for m in offsets] for f in (0, core)]

    own_rows, near_rows = place(0, 4, core), place(1, 6, core)
    far_rows, across_rows = place(2, 7, 0), place(3, 5, 0)
    odd = [n.bit_count() % 2 for n in range(1 << len(lead))]
    far_block, across_block = (far_rows, across_rows), (across_rows, far_rows)
    places = (
        [across_block[o][f][n] for f in (0, 1) for n, o in enumerate(odd)],
        [block[1 - o][n] for block in (own_rows, near_rows) for n, o in enumerate(odd)],
        [far_block[o][f][n] for f in (0, 1) for n, o in enumerate(odd)],
        [block[o][n] for block in (own_rows, near_rows) for n, o in enumerate(odd)],
    )
    blocks = (own, near, far, across, one, two)
    *sends, far, near = stats(blocks, bank_keys, bank_labels.T, places, queries.shape[0])
    far_came, near_came = (swap(send, core) for send in sends)
    for bit in lead[::-1]:
        (send,) = merge(far, far_came, classes, 1, 2, encode)
        (far,) = merge(far, far_came, classes, 0, 1, keep)
        far_came = swap(send, bit ^ core)
        (send,) = merge(near, near_came, classes, 1, 2, encode)
        (near,) = merge(near, near_came, classes, 0, 1, keep)
        near_came = swap(send, bit ^ core)
    (far,) = merge(far, far_came, classes, 0, 2, encode)
    own, near = merge(near, near_came, classes, 0, 2, keep, encode)
    far = swap_far(far)
    near = swap(near, 1)
    across = swap(tail(far), core)
    return finish(add(own, far, classes), near, across, classes)


def solution(mesh):
    placed = P(("groups", "bank", "query"), None)
    query, bank = mesh.shape["query"], mesh.shape["bank"]
    lead = [1 << b for b in range(2, query.bit_length() - 1)]
    lead += [query << b for b in range(1, bank.bit_length() - 1)]
    return jax.shard_map(
        functools.partial(local, query * bank, query, lead),
        mesh=mesh,
        in_specs=(placed,) * 3,
        out_specs=placed,
        check_vma=False,
    )
```
